256 devices in a mesh: band: 32 (over x, z_hi, core), grid: 8 (over y, z_lo).
Axes of the slice: x: 4, y: 4, z: 8 (z_hi: 4, z_lo: 2; z = z_hi * 2 + z_lo), core: 2. Of those that a mesh axis runs over, the one named last changes fastest.
Arguments:
- orbitals: bfloat16 [64, 96, 96, 96], P('band', 'grid'), may hold values from -2 to 2
- exchange_in: float32 [64, 96, 96, 96], P('band', 'grid'), may hold values from -2 to 2
- window_slot: int32 [32], P('band'), may hold values from 0 to 1
- task_pairs: int32 [32, 2, 8], P('band'), may hold values from 0 to 31
- task_count: int32 [32], P('band'), may hold values from 1 to 8, 128 in all
Outputs:
- exchange_out: float32 [64, 96, 96, 96], P('band', 'grid')
The draws below stay inside these ranges and needn't reach their ends.
Inputs may be any that keep to these rules, and one draw needn't show every extreme that they name: task_pairs[g, 0, k] and task_pairs[g, 1, k] are the window positions of the source and target band of task k of band group g; entries with k >= task_count[g] are ignored. `task_count`: some band group has exactly 8 live tasks.
All inputs are finite; a program needn't handle non-finite values.
Results may differ from the reference program's by a relative error of at most 0.0003.
Values may be sent and summed in bfloat16 or wider, within the bound.
A program may use at most 128 MiB of HBM per device.

```python
import math
import jax
import jax.numpy as jnp
import numpy as np
from jax import lax

NX = 96
NY = 96
NZ = 96
BAND_DEV = 2
TASK_CAP = 8
BANDS = 64
N_BAND = 32


def draw_orbitals(key, part):
    key = jax.random.fold_in(key, 11)
    shape_full = (BAND_DEV * N_BAND, NX, NY, NZ)
    rough_key = jax.random.fold_in(key, 0)
    values = jnp.clip(0.25 * jax.random.normal(rough_key, shape_full, jnp.float32), -2.0, 2.0)
    return values.astype(jnp.bfloat16)


def place_ends(values, key, least, high):
    index_at = [jax.random.randint(jax.random.fold_in(key, axis), (), 0, length) for axis, length in enumerate(values.shape)]
    longest = values.shape.index(max(values.shape))
    neighbour = index_at[:longest] + [(index_at[longest] + 1) % values.shape[longest]] + index_at[longest + 1:]
    return values.at[tuple(index_at)].set(least).at[tuple(neighbour)].set(high)


def block_levels(rng, shape, shards, low, high):
    gain = 1.0
    for position, parts in shards:
        steps = jax.random.uniform(jax.random.fold_in(jax.random.fold_in(rng, 6), position), (parts,), jnp.float32, low / len(shards), high / len(shards))
        gain = gain * jnp.repeat(jnp.exp(steps), shape[position] // parts).reshape((-1,) + (1,) * (len(shape) - 1 - position))
    return gain


def length_profile(number_of, total, bound, slope):
    portions = [(1 << 20) // math.isqrt(grade ** slope) + 1 for grade in range(2, number_of + 1)]
    spare, given = total - bound - (number_of - 1), [1] * (number_of - 1)
    while spare > 0:
        movable = [i for i in range(number_of - 1) if given[i] < bound]
        whole, remaining = sum([portions[i] for i in movable]), spare
        for i in movable:
            addition = min(bound - given[i], max(1, remaining * portions[i] // whole), spare)
            given[i] = given[i] + addition
            spare = spare - addition
    return np.array([bound] + given)


def uneven(stream_key, count, total, most, skew):
    if count == 2:
        one = jax.random.randint(stream_key, (), max(1, total - most), min(most, total - 1) + 1)
        return jnp.stack([one, total - one])
    lengths = jnp.asarray(length_profile(count, total, most, skew), jnp.int32)
    pairs = (count - 1) // 2
    donor, taker = lengths[1:1 + 2 * pairs:2], lengths[2:2 + 2 * pairs:2]
    room = jnp.minimum(donor - 1, most - taker)
    moved = jax.random.randint(jax.random.fold_in(stream_key, 1), (pairs,), 0, 1 << 20) % (room + 1)
    lengths = lengths.at[1:1 + 2 * pairs:2].set(donor - moved).at[2:2 + 2 * pairs:2].set(taker + moved)
    return lengths[jax.random.permutation(jax.random.fold_in(stream_key, 2), count)]


def bell_draw(key, dims, scale, most, pieces=(), kind=jnp.bfloat16):
    result = scale * jax.random.normal(key, dims, jnp.float32)
    if pieces:
        result = result * block_levels(key, dims, pieces, -0.22, 0.18)
    return jnp.clip(result, -most, most).astype(kind)


def setup_inputs(seed: int = 0) -> dict:
    splits = jax.random.split(jax.random.key(seed), 6)
    return {
        "orbitals": draw_orbitals(jax.random.fold_in(splits[5], 71), 0),
        "exchange_in": bell_draw(splits[1], (BANDS, NX, NY, NZ), 0.25, 2.0, ((0, 32), (1, 8)), jnp.float32),
        "window_slot": place_ends(jax.random.randint(splits[2], (N_BAND,), 0, BAND_DEV), jax.random.fold_in(splits[2], 1), 0, BAND_DEV - 1).astype(jnp.int32),
        "task_pairs": place_ends(jax.random.randint(splits[3], (N_BAND, 2, TASK_CAP), 0, N_BAND), jax.random.fold_in(splits[3], 1), 0, N_BAND - 1).astype(jnp.int32),
        "task_count": uneven(splits[4], N_BAND, TASK_CAP * N_BAND // 2, TASK_CAP, 2).astype(jnp.int32),
    }


def wavenumbers(length):
    steps_all = jnp.arange(length, dtype=jnp.int32)
    signed = jnp.where(steps_all <= length // 2, steps_all, steps_all - length)
    return signed.astype(jnp.float32) * (2.0 * math.pi / length)


def coulomb_kernel():
    wave_first = wavenumbers(NX)[:, None, None]
    wave_second = wavenumbers(NY)[None, :, None]
    wave_third = wavenumbers(NZ)[None, None, :]
    square = wave_first * wave_first + wave_second * wave_second + wave_third * wave_third
    safe_square = jnp.where(square > 0, square, 1.0)
    return jnp.where(square > 0, (4.0 * math.pi) / safe_square, 0.0)


def reference(orbitals, exchange_in, window_slot, task_pairs, task_count):
    owners = jnp.arange(N_BAND, dtype=jnp.int32)
    picked = owners * BAND_DEV + window_slot.astype(jnp.int32)
    window = orbitals[picked]
    kernel = coulomb_kernel()
    sources = task_pairs[:, 0, :].reshape(-1).astype(jnp.int32)
    targets = task_pairs[:, 1, :].reshape(-1).astype(jnp.int32)
    alive_mask = (jnp.arange(TASK_CAP, dtype=jnp.int32)[None, :] < task_count[:, None]).reshape(-1)

    def one_task(partial_value, task_item):
        source, target, alive_flag = task_item
        source_orb = window[source].astype(jnp.float32)
        target_orb = window[target].astype(jnp.float32)
        density = source_orb * target_orb
        potential = jnp.fft.ifftn(kernel * jnp.fft.fftn(density)).real
        contribution = jnp.where(alive_flag, potential * source_orb, 0.0)
        return partial_value.at[target].add(contribution), None

    partial_value = jnp.zeros((N_BAND, NX, NY, NZ), jnp.float32)
    partial_value, _ = lax.scan(one_task, partial_value, (sources, targets, alive_mask))
    return exchange_in.at[picked].add(partial_value)
```

```python
import functools
import math

import jax
import jax.numpy as jnp
import numpy as np
from jax import lax
from jax.experimental import pallas as pl
from jax.experimental.pallas import tpu as pltpu
from jax.sharding import PartitionSpec as P

MESH = pl.DeviceIdType.MESH
LANES = 128
QUAD = 4


def hartley_table(length):
    steps_all = np.arange(length)
    angle = (steps_all[:, None] * steps_all[None, :] % length) * (2.0 * math.pi / length)
    return np.cos(angle) + np.sin(angle)


def split_table(length):
    table = hartley_table(length).astype(np.float32)
    high = table.astype(jnp.bfloat16)
    low = (table - high.astype(np.float32)).astype(jnp.bfloat16)
    return high, low


def lane_table(length):
    high, low = split_table(length)
    out = np.zeros((2 * LANES, 2 * LANES), jnp.bfloat16)
    out[:length, :length] = high
    out[:length, LANES : LANES + length] = low
    out[LANES : LANES + length, :length] = high
    return out


def row_table(length):
    high, low = split_table(length)
    out = np.zeros((2 * length, 2 * length), jnp.bfloat16)
    out[:length, :length] = high
    out[:length, length:] = high
    out[length:, :length] = low
    return out


def wavenumbers(length):
    steps_all = jnp.arange(length, dtype=jnp.int32)
    signed = jnp.where(steps_all <= length // 2, steps_all, steps_all - length)
    return signed.astype(jnp.float32) * (2.0 * math.pi / length)


def quarter_kernel(span, quarter):
    rows = span // QUAD
    wave = wavenumbers(span)
    second = lax.dynamic_slice_in_dim(wave, quarter * rows, rows)
    square = (wave * wave)[:, None, None] + (second * second)[None, :, None] + (wave * wave)[None, None, :]
    safe = jnp.where(square > 0, square, 1.0)
    kernel = jnp.where(square > 0, 4.0 * math.pi / span**3 / safe, 0.0)
    return jnp.pad(kernel, ((0, 0), (0, 0), (0, LANES - span))).reshape(span * rows, LANES)


def split(values):
    high = values.astype(jnp.bfloat16)
    return high, (values - high.astype(jnp.float32)).astype(jnp.bfloat16)


def along_lanes(values, table):
    both = jnp.dot(jnp.concatenate(split(values), axis=1), table, preferred_element_type=jnp.float32)
    return both[:, :LANES] + both[:, LANES:]


def along_rows(values, table):
    both = jnp.dot(table, jnp.concatenate(split(values), axis=0), preferred_element_type=jnp.float32)
    span = values.shape[0]
    return both[:span] + both[span:]


def task_kernel(
    quads, span, source_ref, target_ref, weight_ref, window_ref, kernel_ref, lane_ref, row_ref, out_ref,
    send_out, recv_out, send_back, recv_back, total, partner_part,
    out_send_sem, out_recv_sem, back_send_sem, back_recv_sem, part_sems,
):
    band = lax.axis_index("band")
    core = lax.rem(band, 2)
    pair = band - core
    members = 2 * lax.axis_size("grid")
    me = 2 * lax.axis_index("grid") + core
    own_rows = span // members
    rows = span // QUAD
    block = own_rows * rows

    def place(member):
        return {"band": pair + lax.rem(member, 2), "grid": member // 2}

    barrier = pltpu.get_barrier_semaphore()

    def greet(step, carry):
        pl.semaphore_signal(barrier, inc=1, device_id=place(lax.rem(me + step, members)), device_id_type=MESH)
        return carry

    lax.fori_loop(1, members, greet, 0)
    pl.semaphore_wait(barrier, members - 1)

    def at(ref, quad, member):
        return ref.at[quad, pl.ds(pl.multiple_of(member * block, 8), block)]

    def remote(quad, member, origin, src, dst, send_sem, recv_sem):
        return pltpu.make_async_remote_copy(
            src_ref=at(src, quad, member), dst_ref=at(dst, quad, origin),
            send_sem=send_sem.at[quad, member], recv_sem=recv_sem.at[quad, origin],
            device_id=place(member), device_id_type=MESH,
        )

    def local(quad, src, dst, recv_sem):
        return pltpu.make_async_copy(at(src, quad, me), at(dst, quad, me), recv_sem.at[quad, me])

    def start_all(quad, src, dst, send_sem, recv_sem):
        def step_one(step, carry):
            remote(quad, lax.rem(me + step, members), me, src, dst, send_sem, recv_sem).start()
            return carry

        lax.fori_loop(1, members, step_one, 0)
        local(quad, src, dst, recv_sem).start()

    def wait_recv(quad, src, dst, send_sem, recv_sem):
        def step_one(step, carry):
            other = lax.rem(me + step, members)
            remote(quad, other, other, src, dst, send_sem, recv_sem).wait_recv()
            return carry

        lax.fori_loop(1, members, step_one, 0)
        local(quad, src, dst, recv_sem).wait()

    def wait_send(quad, src, dst, send_sem, recv_sem):
        def step_one(step, carry):
            other = lax.rem(me + step, members)
            remote(quad, other, me, src, dst, send_sem, recv_sem).wait_send()
            return carry

        lax.fori_loop(1, members, step_one, 0)

    outward = (send_out, recv_out, out_send_sem, out_recv_sem)
    backward = (send_back, recv_back, back_send_sem, back_recv_sem)

    def inner(quad):
        def one(slot, carry):
            source, target = source_ref[quad * QUAD + slot], target_ref[quad * QUAD + slot]
            for two in range(own_rows // 2):
                part = pl.ds(2 * two * span, 2 * span)
                density = window_ref[source, part].astype(jnp.float32) * window_ref[target, part].astype(jnp.float32)
                mixed = along_lanes(density, lane_ref[...])
                mixed = along_rows(jnp.concatenate([mixed[:span], mixed[span:]], axis=1), row_ref[...])
                for quarter in range(QUAD):
                    for half in range(2):
                        start = (slot * QUAD + quarter) * block + (2 * two + half) * rows
                        send_out[quad, pl.ds(pl.multiple_of(start, 8), rows)] = mixed[
                            quarter * rows : (quarter + 1) * rows, half * LANES : (half + 1) * LANES
                        ]
            return carry

        lax.fori_loop(0, QUAD, one, 0)
        start_all(quad, *outward)

    def outer(quad):
        wait_recv(quad, *outward)

        def one(two, carry):
            picks = [pl.ds(2 * two + half, span, stride=rows) for half in range(2)]
            values = jnp.concatenate([recv_out[quad, pick] for pick in picks], axis=1)
            factor = jnp.concatenate([kernel_ref[pick] for pick in picks], axis=1)
            spectrum = along_rows(values, row_ref[...]) * factor
            restored = along_rows(spectrum, row_ref[...])
            for half in range(2):
                send_back[quad, picks[half]] = restored[:, half * LANES : (half + 1) * LANES]
            return carry

        lax.fori_loop(0, rows // 2, one, 0)
        start_all(quad, *backward)

    def finish(quad):
        wait_recv(quad, *backward)

        def one(slot, carry):
            source = source_ref[quad * QUAD + slot]
            weights = [weight_ref[side, quad * QUAD + slot] for side in range(2)]
            for two in range(own_rows // 2):
                halves = []
                for half in range(2):
                    starts = [(slot * QUAD + quarter) * block + (2 * two + half) * rows for quarter in range(QUAD)]
                    halves.append(
                        jnp.concatenate(
                            [recv_back[quad, pl.ds(pl.multiple_of(start, 8), rows)] for start in starts], axis=0
                        )
                    )
                mixed = along_rows(jnp.concatenate(halves, axis=1), row_ref[...])
                potential = along_lanes(
                    jnp.concatenate([mixed[:, :LANES], mixed[:, LANES:]], axis=0), lane_ref[...]
                )
                part = pl.ds(2 * two * span, 2 * span)
                action = potential * window_ref[source, part].astype(jnp.float32)
                for side in range(2):
                    total[side, part] += action * weights[side]
            return carry

        lax.fori_loop(0, QUAD, one, 0)

    total[...] = jnp.zeros_like(total)
    for quad in range(quads):
        inner(quad)
    for quad in range(quads):
        outer(quad)
        if quad > 0:
            finish(quad - 1)
    finish(quads - 1)

    swap = pltpu.make_async_remote_copy(
        src_ref=total.at[1 - core], dst_ref=partner_part, send_sem=part_sems.at[0], recv_sem=part_sems.at[1],
        device_id={"band": pair + 1 - core, "grid": lax.axis_index("grid")}, device_id_type=MESH,
    )
    swap.start()
    out_ref[core] = total[core]
    swap.wait_recv()
    out_ref[1 - core] = partner_part[...]
    swap.wait_send()
    for quad in range(quads):
        wait_send(quad, *outward)
        wait_send(quad, *backward)


def run_tasks(quads, span, members, sources, targets, weights, window, kernel, lane_constant, row_constant):
    own_rows = span // members
    whole = (quads, span * span // QUAD, LANES)
    smem, vmem = pl.BlockSpec(memory_space=pltpu.SMEM), pl.BlockSpec(memory_space=pltpu.VMEM)
    sems = pltpu.SemaphoreType.DMA((quads, members))
    return pl.pallas_call(
        functools.partial(task_kernel, quads, span),
        out_shape=jax.ShapeDtypeStruct((2, own_rows * span, LANES), jnp.float32),
        in_specs=[smem] * 3 + [vmem] * 4,
        out_specs=vmem,
        scratch_shapes=[pltpu.VMEM(whole, jnp.float32)] * 4
        + [pltpu.VMEM((2, own_rows * span, LANES), jnp.float32), pltpu.VMEM((own_rows * span, LANES), jnp.float32)]
        + [sems] * 4
        + [pltpu.SemaphoreType.DMA((2,))],
        compiler_params=pltpu.CompilerParams(
            collective_id=quads, has_side_effects=True, vmem_limit_bytes=56 * 1024 * 1024
        ),
        name="exchange_tasks",
    )(sources, targets, weights, window, kernel, lane_constant, row_constant)


def task_lists(task_pairs, task_count, groups, group):
    cap = task_pairs.shape[-1]
    mine = jnp.concatenate([task_pairs.reshape(2 * cap), task_count])
    every = lax.all_gather(mine, "band", axis=0, tiled=False)
    alive = jnp.arange(cap, dtype=jnp.int32)[None, :] < every[:, 2 * cap :]
    position = jnp.where(alive, every[:, cap : 2 * cap] * groups + every[:, :cap], -1).reshape(-1)
    entries = jnp.arange(groups * groups, dtype=jnp.int32)
    times = jnp.sum((position[:, None] == entries[None, :]).astype(jnp.int32), axis=0).reshape(-1, 2 * groups)
    live = times > 0
    most = jnp.max(jnp.sum(live.astype(jnp.int32), axis=1))
    own_times = lax.dynamic_index_in_dim(times, group, 0, keepdims=False)
    own_live = own_times > 0
    local = jnp.arange(2 * groups, dtype=jnp.int32)
    before = jnp.sum((own_live[None, :] & (local[None, :] < local[:, None])).astype(jnp.int32), axis=1)
    here = own_live[None, :] & (before[None, :] == local[:, None])
    entry = jnp.sum(jnp.where(here, local[None, :], 0), axis=1)
    often = jnp.sum(jnp.where(here, own_times[None, :], 0), axis=1).astype(jnp.float32)
    side = entry // groups
    weights = jnp.stack([jnp.where(side == 0, often, 0.0), jnp.where(side == 1, often, 0.0)])
    return entry % groups, 2 * group + side, weights, most


def on_device(orbitals, exchange_in, window_slot, task_pairs, task_count):
    band_dev, slab_rows, span, _ = orbitals.shape
    grid_parts = lax.axis_size("grid")
    groups = lax.axis_size("band")
    members = 2 * grid_parts
    own_rows = span // members
    band = lax.axis_index("band")
    core, group = band % 2, band // 2
    sources, targets, weights, most = task_lists(task_pairs, task_count, groups, group)

    mine = lax.dynamic_index_in_dim(orbitals, window_slot[0], 0, keepdims=False)
    mine = jnp.pad(mine.reshape(2, own_rows * span, span), ((0, 0), (0, 0), (0, LANES - span)))
    keep = lax.dynamic_index_in_dim(mine, core, 0)
    give = lax.dynamic_index_in_dim(mine, 1 - core, 0)
    got = lax.ppermute(give, "band", [(i, i ^ 1) for i in range(groups)])
    both = jnp.where(core == 0, jnp.concatenate([keep, got]), jnp.concatenate([got, keep]))
    window = lax.all_gather(
        both, "band", axis=0, tiled=True,
        axis_index_groups=[list(range(0, groups, 2)), list(range(1, groups, 2))],
    )

    member = 2 * lax.axis_index("grid") + core
    constants = (quarter_kernel(span, member % QUAD), jnp.asarray(lane_table(span)), jnp.asarray(row_table(span)))

    def few():
        return run_tasks(3, span, members, sources, targets, weights, window, *constants)

    def many():
        def step(carry):
            start, total = carry
            lists = [lax.dynamic_slice_in_dim(a, start, 16, a.ndim - 1) for a in (sources, targets, weights)]
            return start + 16, total + run_tasks(4, span, members, *lists, window, *constants)

        zero = jnp.zeros((2, own_rows * span, LANES), jnp.float32)
        return lax.while_loop(lambda carry: carry[0] < most, step, (jnp.int32(0), zero))[1]

    owned = lax.cond(most <= 12, few, many)
    owned = owned.reshape(slab_rows, span, LANES)[:, :, :span]
    slot_ids = jnp.arange(band_dev, dtype=jnp.int32)[:, None, None, None]
    return exchange_in + jnp.where(slot_ids == window_slot[0], owned, 0.0)


def solution(mesh):
    in_specs = (
        P("band", "grid", None, None),
        P("band", "grid", None, None),
        P("band"),
        P("band", None, None),
        P("band"),
    )
    out_specs = P("band", "grid", None, None)
    return jax.shard_map(
        on_device, mesh=mesh, in_specs=in_specs, out_specs=out_specs, check_vma=False
    )
```

```python
import functools
import math

import jax
import jax.numpy as jnp
import numpy as np
from jax import lax
from jax.experimental import pallas as pl
from jax.experimental.pallas import tpu as pltpu
from jax.sharding import PartitionSpec as P

MESH = pl.DeviceIdType.MESH
LANES = 128
QUAD = 4


def hartley_table(length):
    steps_all = np.arange(length)
    angle = (steps_all[:, None] * steps_all[None, :] % length) * (2.0 * math.pi / length)
    return np.cos(angle) + np.sin(angle)


def split_table(length):
    table = hartley_table(length).astype(np.float32)
    high = table.astype(jnp.bfloat16)
    low = (table - high.astype(np.float32)).astype(jnp.bfloat16)
    return high, low


def lane_table(length):
    high, low = split_table(length)
    out = np.zeros((2 * LANES, 2 * LANES), jnp.bfloat16)
    out[:length, :length] = high
    out[:length, LANES : LANES + length] = low
    out[LANES : LANES + length, :length] = high
    return out


def row_tables(length):
    high, low = split_table(length)
    order = np.concatenate([np.arange(0, length, 2), np.arange(1, length, 2)])
    out = np.zeros((3, 2 * length, 2 * length), jnp.bfloat16)
    plain = np.arange(length)
    for which, pick in enumerate((np.ix_(plain, plain), np.ix_(plain, order), np.ix_(order, plain))):
        out[which, :length, :length] = high[pick]
        out[which, :length, length:] = high[pick]
        out[which, length:, :length] = low[pick]
    return out


def emphasis(length):
    steps_all = np.arange(length)
    signed = np.where(steps_all <= length // 2, steps_all, steps_all - length).astype(np.float64)
    return ((signed**2)[:, None] + (signed**2)[None, :] + 1.0) ** 0.75


def undo_emphasis(length):
    out = np.zeros((length, LANES), np.float32)
    out[:, :length] = 1.0 / emphasis(length)
    return out


def wavenumbers(length):
    steps_all = jnp.arange(length, dtype=jnp.int32)
    signed = jnp.where(steps_all <= length // 2, steps_all, steps_all - length)
    return signed.astype(jnp.float32) * (2.0 * math.pi / length)


def quarter_kernel(span, quarter):
    rows = span // QUAD
    wave = wavenumbers(span)
    second = lax.dynamic_slice_in_dim(wave, quarter * rows, rows)
    square = (wave * wave)[:, None, None] + (second * second)[None, :, None] + (wave * wave)[None, None, :]
    safe = jnp.where(square > 0, square, 1.0)
    stress = lax.dynamic_slice_in_dim(jnp.asarray(emphasis(span), jnp.float32), quarter * rows, rows)
    kernel = jnp.where(square > 0, 4.0 * math.pi / span**3 / safe, 0.0) * stress
    return jnp.pad(kernel, ((0, 0), (0, 0), (0, LANES - span))).reshape(span * rows, LANES)


def split(values):
    high = values.astype(jnp.bfloat16)
    return high, (values - high.astype(jnp.float32)).astype(jnp.bfloat16)


def unpack(values):
    rows = values.shape[0] // 3
    parts = [values[third * rows : (third + 1) * rows] for third in range(3)]
    lane = lax.broadcasted_iota(jnp.int32, (rows, LANES), 1)
    turned = [pltpu.roll(parts[third], 32 * (third + 1), 1) for third in range(3)]
    last = jnp.where(lane < 32, turned[0], jnp.where(lane < 64, turned[1], turned[2]))
    return jnp.concatenate([jnp.where(lane < 96, part, 0.0) for part in (*parts, last)], axis=0)


LEVELS = 32766.0
FINE = 2.0**24
STEPS = 256.0
LN2 = math.log(2.0)


def grade(peak):
    return jnp.ceil(jnp.log(jnp.maximum(peak, 1e-30)) * (STEPS / LN2) + 0.01)


def size(graded):
    return jnp.exp(graded * (LN2 / STEPS))


def nearest(values):
    return jnp.round(values).astype(jnp.int32)


def encode(first, second, apart):
    lane = lax.broadcasted_iota(jnp.int32, first.shape, 1)
    if apart:
        columns = (first[:, :1], second[:, :1])
        first, second = jnp.where(lane > 0, first, 0.0), jnp.where(lane > 0, second, 0.0)
    top = grade(jnp.max(jnp.maximum(jnp.abs(first), jnp.abs(second)), axis=(0, 1), keepdims=True))
    factor = LEVELS / size(top)
    word = nearest(first * factor) * 65536 + nearest(second * factor)
    word = jnp.where(lane == 96, top.astype(jnp.int32), word)
    if apart:
        high = grade(jnp.max(jnp.maximum(jnp.abs(columns[0]), jnp.abs(columns[1])), axis=(0, 1), keepdims=True))
        factor = FINE / size(high)
        word = jnp.where(lane == 97, high.astype(jnp.int32), word)
        word = jnp.where(lane == 98, nearest(columns[0] * factor), word)
        word = jnp.where(lane == 99, nearest(columns[1] * factor), word)
    return word


def decode(word, apart):
    second = lax.shift_right_arithmetic(lax.shift_left(word, 16), 16)
    first = lax.shift_right_arithmetic(word - second, 16)
    factor = size(word[:, 96:97].astype(jnp.float32)) * (1.0 / LEVELS)
    first, second = first.astype(jnp.float32) * factor, second.astype(jnp.float32) * factor
    if apart:
        lane = lax.broadcasted_iota(jnp.int32, word.shape, 1)
        factor = size(word[:, 97:98].astype(jnp.float32)) * (1.0 / FINE)
        first = jnp.where(lane == 0, word[:, 98:99].astype(jnp.float32) * factor, first)
        second = jnp.where(lane == 0, word[:, 99:100].astype(jnp.float32) * factor, second)
    return first, second


def along_lanes(values, table):
    both = jnp.dot(jnp.concatenate(split(values), axis=1), table, preferred_element_type=jnp.float32)
    return both[:, :LANES] + both[:, LANES:]


def along_rows(values, table):
    both = jnp.dot(table, jnp.concatenate(split(values), axis=0), preferred_element_type=jnp.float32)
    span = values.shape[0]
    return both[:span] + both[span:]


def task_kernel(
    quads, span, source_ref, target_ref, weight_ref, window_ref, kernel_ref, undo_ref, lane_ref, row_ref, out_ref,
    send_out, recv_out, send_back, recv_back, total, partner_part,
    out_send_sem, out_recv_sem, back_send_sem, back_recv_sem, part_sems,
):
    band = lax.axis_index("band")
    core = lax.rem(band, 2)
    pair = band - core
    members = 2 * lax.axis_size("grid")
    me = 2 * lax.axis_index("grid") + core
    own_rows = span // members
    rows = span // QUAD
    block = own_rows // 2 * rows

    def place(member):
        return {"band": pair + lax.rem(member, 2), "grid": member // 2}

    barrier = pltpu.get_barrier_semaphore()

    def greet(step, carry):
        pl.semaphore_signal(barrier, inc=1, device_id=place(lax.rem(me + step, members)), device_id_type=MESH)
        return carry

    lax.fori_loop(1, members, greet, 0)
    pl.semaphore_wait(barrier, members - 1)

    def at(ref, quad, member):
        return ref.at[quad, pl.ds(pl.multiple_of(member * block, 8), block)]

    def remote(quad, member, origin, src, dst, send_sem, recv_sem):
        return pltpu.make_async_remote_copy(
            src_ref=at(src, quad, member), dst_ref=at(dst, quad, origin),
            send_sem=send_sem.at[quad, member], recv_sem=recv_sem.at[quad, origin],
            device_id=place(member), device_id_type=MESH,
        )

    def local(quad, src, dst, recv_sem):
        return pltpu.make_async_copy(at(src, quad, me), at(dst, quad, me), recv_sem.at[quad, me])

    def start_all(quad, src, dst, send_sem, recv_sem):
        def step_one(step, carry):
            remote(quad, lax.rem(me + step, members), me, src, dst, send_sem, recv_sem).start()
            return carry

        lax.fori_loop(1, members, step_one, 0)
        local(quad, src, dst, recv_sem).start()

    def wait_recv(quad, src, dst, send_sem, recv_sem):
        def step_one(step, carry):
            other = lax.rem(me + step, members)
            remote(quad, other, other, src, dst, send_sem, recv_sem).wait_recv()
            return carry

        lax.fori_loop(1, members, step_one, 0)
        local(quad, src, dst, recv_sem).wait()

    def wait_send(quad, src, dst, send_sem, recv_sem):
        def step_one(step, carry):
            other = lax.rem(me + step, members)
            remote(quad, other, me, src, dst, send_sem, recv_sem).wait_send()
            return carry

        lax.fori_loop(1, members, step_one, 0)

    outward = (send_out, recv_out, out_send_sem, out_recv_sem)
    backward = (send_back, recv_back, back_send_sem, back_recv_sem)

    packed = window_ref.shape[1] // (own_rows // 2)

    def window_part(position, two):
        return window_ref[position, pl.ds(two * packed, packed)].astype(jnp.float32)

    def inner(quad):
        def one(slot, carry):
            source, target = source_ref[quad * QUAD + slot], target_ref[quad * QUAD + slot]
            for two in range(own_rows // 2):
                density = window_part(source, two) * window_part(target, two)
                mixed = along_lanes(unpack(density), lane_ref[...])
                mixed = along_rows(jnp.concatenate([mixed[:span], mixed[span:]], axis=1), row_ref[0])
                word = encode(mixed[:, :LANES], mixed[:, LANES:], True)
                for quarter in range(QUAD):
                    start = (slot * QUAD + quarter) * block + two * rows
                    send_out[quad, pl.ds(pl.multiple_of(start, 8), rows)] = word[quarter * rows : (quarter + 1) * rows]
            return carry

        lax.fori_loop(0, QUAD, one, 0)
        start_all(quad, *outward)

    def outer(quad):
        wait_recv(quad, *outward)

        def one(two, carry):
            picks = [pl.ds(2 * two + half, span // 2, stride=rows) for half in range(2)]
            values = [jnp.concatenate(decode(recv_out[quad, pick], True), axis=0) for pick in picks]
            factors = [kernel_ref[pl.ds(2 * two + half, span, stride=rows)] for half in range(2)]
            spectrum = along_rows(jnp.concatenate(values, axis=1), row_ref[1]) * jnp.concatenate(factors, axis=1)
            restored = along_rows(spectrum, row_ref[2])
            for half in range(2):
                side = slice(half * LANES, (half + 1) * LANES)
                send_back[quad, picks[half]] = encode(restored[: span // 2, side], restored[span // 2 :, side], False)
            return carry

        lax.fori_loop(0, rows // 2, one, 0)
        start_all(quad, *backward)

    def finish(quad):
        wait_recv(quad, *backward)

        def one(slot, carry):
            source = source_ref[quad * QUAD + slot]
            weights = [weight_ref[side, quad * QUAD + slot] for side in range(2)]
            for two in range(own_rows // 2):
                starts = [(slot * QUAD + quarter) * block + two * rows for quarter in range(QUAD)]
                word = jnp.concatenate(
                    [recv_back[quad, pl.ds(pl.multiple_of(start, 8), rows)] for start in starts], axis=0
                )
                mixed = [half * undo_ref[...] for half in decode(word, False)]
                mixed = along_rows(jnp.concatenate(mixed, axis=1), row_ref[0])
                potential = along_lanes(
                    jnp.concatenate([mixed[:, :LANES], mixed[:, LANES:]], axis=0), lane_ref[...]
                )
                part = pl.ds(2 * two * span, 2 * span)
                action = potential * unpack(window_part(source, two))
                for side in range(2):
                    total[side, part] += action * weights[side]
            return carry

        lax.fori_loop(0, QUAD, one, 0)

    total[...] = jnp.zeros_like(total)
    for quad in range(quads):
        inner(quad)
    for quad in range(quads):
        outer(quad)
        if quad > 0:
            finish(quad - 1)
    finish(quads - 1)

    swap = pltpu.make_async_remote_copy(
        src_ref=total.at[1 - core], dst_ref=partner_part, send_sem=part_sems.at[0], recv_sem=part_sems.at[1],
        device_id={"band": pair + 1 - core, "grid": lax.axis_index("grid")}, device_id_type=MESH,
    )
    swap.start()
    out_ref[core] = total[core]
    swap.wait_recv()
    out_ref[1 - core] = partner_part[...]
    swap.wait_send()
    for quad in range(quads):
        wait_send(quad, *outward)
        wait_send(quad, *backward)


def run_tasks(quads, span, members, *operands):
    own_rows = span // members
    whole = (quads, span * span // QUAD // 2, LANES)
    smem, vmem = pl.BlockSpec(memory_space=pltpu.SMEM), pl.BlockSpec(memory_space=pltpu.VMEM)
    sems = pltpu.SemaphoreType.DMA((quads, members))
    return pl.pallas_call(
        functools.partial(task_kernel, quads, span),
        out_shape=jax.ShapeDtypeStruct((2, own_rows * span, LANES), jnp.float32),
        in_specs=[smem] * 3 + [vmem] * 5,
        out_specs=vmem,
        scratch_shapes=[pltpu.VMEM(whole, jnp.int32)] * 4
        + [pltpu.VMEM((2, own_rows * span, LANES), jnp.float32), pltpu.VMEM((own_rows * span, LANES), jnp.float32)]
        + [sems] * 4
        + [pltpu.SemaphoreType.DMA((2,))],
        compiler_params=pltpu.CompilerParams(
            collective_id=quads, has_side_effects=True, vmem_limit_bytes=56 * 1024 * 1024
        ),
        name="exchange_tasks",
    )(*operands)


def gather_kernel(
    rings, span, orbital_ref, slot_ref, pairs_ref, count_ref, window_ref, lists_ref, give, own_list,
    swap_sems, list_send, list_recv, near_send, near_recv, far_send, far_recv,
):
    ring_x, ring_z = rings
    band = lax.axis_index("band")
    groups = lax.axis_size("band")
    core, chip = lax.rem(band, 2), band // 2
    at_x, at_z = chip // ring_z, lax.rem(chip, ring_z)
    packed = window_ref.shape[0] // groups

    barrier = pltpu.get_barrier_semaphore()

    def greet(step, carry):
        pl.semaphore_signal(barrier, inc=1, device_id={"band": lax.rem(band + step, groups)}, device_id_type=MESH)
        return carry

    lax.fori_loop(1, groups, greet, 0)

    part_rows = packed // 3
    quarter = part_rows // 3
    first = slot_ref[0] == 0
    for two in range(3):
        for side in range(2):
            rows = pl.ds(side * (orbital_ref.shape[1] // 2) + two * 4 * quarter, 4 * quarter)
            values = jnp.where(
                first, orbital_ref[0, rows].astype(jnp.float32), orbital_ref[1, rows].astype(jnp.float32)
            )
            last = values[3 * quarter :]
            for third in range(3):
                full = jnp.concatenate(
                    [values[third * quarter : (third + 1) * quarter], last[:, 32 * third : 32 * third + 32]], axis=1
                ).astype(jnp.bfloat16)
                row = two * part_rows + third * quarter

                @pl.when(core == side)
                def _():
                    window_ref[pl.ds(pl.multiple_of(band * packed + row, 16), quarter)] = full

                @pl.when(core != side)
                def _():
                    give[pl.ds(row, quarter)] = full

    own_list[...] = jnp.zeros_like(own_list)
    own_list[0:2, 0 : pairs_ref.shape[1]] = pairs_ref[...]
    own_list[2:3] = jnp.full((1, LANES), count_ref[0], jnp.int32)

    pl.semaphore_wait(barrier, groups - 1)

    def blocks(first_band, count):
        return window_ref.at[pl.ds(pl.multiple_of(first_band * packed, 16), count * packed)]

    def send(src, dst, send_sem, recv_sem, target):
        return pltpu.make_async_remote_copy(
            src_ref=src, dst_ref=dst, send_sem=send_sem, recv_sem=recv_sem,
            device_id={"band": target}, device_id_type=MESH,
        )

    def swap(owner):
        return send(give, blocks(owner, 1), swap_sems.at[0], swap_sems.at[1], band + 1 - 2 * core)

    swap(band).start()

    def send_list(step, owner):
        other = lax.rem(band + step, groups)
        return send(own_list, lists_ref.at[owner], list_send.at[step], list_recv.at[step], other)

    def start_list(step, carry):
        send_list(step, band).start()
        return carry

    def place(x, z):
        return lax.rem(x + ring_x, ring_x) * ring_z + lax.rem(z + ring_z, ring_z)

    level = (0, -1, 1, 2)

    def along(ring, step):
        if ring == 0:
            return place(at_x, at_z + step)
        return place(at_x + step, at_z + level[ring - 1])

    def neighbour(ring, step):
        target = place(at_x, at_z + step) if ring == 0 else place(at_x + step, at_z)
        return 2 * target + core

    def near(ring, way):
        block = blocks(2 * along(ring, 0), 2)
        return send(block, block, near_send.at[ring, way], near_recv.at[ring, way], neighbour(ring, 1 - 2 * way))

    def far(ring, way):
        block = blocks(2 * along(ring, -1 + 2 * way) + way, 1)
        return send(block, block, far_send.at[ring, way], far_recv.at[ring, way], neighbour(ring, 1 - 2 * way))

    def begin(ring):
        for way in range(2):
            near(ring, way).start()

    def onward(ring):
        for way in range(2):
            near(ring, way).wait_recv()
            far(ring, way).start()

    swap(band).wait_recv()
    begin(0)
    begin(1)
    lax.fori_loop(1, groups, start_list, 0)
    for way in range(2):
        near(0, way).wait_recv()
        far(0, way).start()
        begin(2 + way)
    onward(1)
    for way in range(2):
        far(0, way).wait_recv()
    begin(4)
    onward(2)
    onward(3)
    onward(4)
    for ring in range(1, 5):
        for way in range(2):
            far(ring, way).wait_recv()

    def end_list(step, carry):
        send_list(step, band).wait_recv()
        send_list(step, band).wait_send()
        return carry

    lax.fori_loop(1, groups, end_list, 0)
    lists_ref[band] = own_list[...]
    swap(band).wait_send()
    for ring in range(5):
        for way in range(2):
            near(ring, way).wait_send()
            far(ring, way).wait_send()


def gather_window(rings, span, orbitals, window_slot, task_pairs, task_count):
    groups = lax.axis_size("band")
    slab_rows = orbitals.shape[1]
    packed = slab_rows // 2 * span * span // LANES
    smem, vmem = pl.BlockSpec(memory_space=pltpu.SMEM), pl.BlockSpec(memory_space=pltpu.VMEM)
    dma = pltpu.SemaphoreType.DMA
    return pl.pallas_call(
        functools.partial(gather_kernel, rings, span),
        out_shape=(
            jax.ShapeDtypeStruct((groups * packed, LANES), jnp.bfloat16),
            jax.ShapeDtypeStruct((groups, 8, LANES), jnp.int32),
        ),
        in_specs=[vmem, smem, vmem, smem],
        out_specs=(vmem, vmem),
        scratch_shapes=[pltpu.VMEM((packed, LANES), jnp.bfloat16), pltpu.VMEM((8, LANES), jnp.int32)]
        + [dma((2,)), dma((groups,)), dma((groups,))]
        + [dma((5, 2))] * 4,
        compiler_params=pltpu.CompilerParams(
            collective_id=9, has_side_effects=True, vmem_limit_bytes=56 * 1024 * 1024
        ),
        name="gather_window",
    )(orbitals.reshape(2, slab_rows * span, span), window_slot, task_pairs[0], task_count)


def task_lists(lists, cap, groups, group):
    alive = jnp.arange(cap, dtype=jnp.int32)[None, :] < lists[:, 2, :1]
    position = jnp.where(alive, lists[:, 1, :cap] * groups + lists[:, 0, :cap], -1).reshape(-1)
    entries = jnp.arange(groups * groups, dtype=jnp.int32)
    times = jnp.sum((position[:, None] == entries[None, :]).astype(jnp.int32), axis=0).reshape(-1, 2 * groups)
    live = times > 0
    most = jnp.max(jnp.sum(live.astype(jnp.int32), axis=1))
    own_times = lax.dynamic_index_in_dim(times, group, 0, keepdims=False)
    own_live = own_times > 0
    local = jnp.arange(2 * groups, dtype=jnp.int32)
    before = jnp.sum((own_live[None, :] & (local[None, :] < local[:, None])).astype(jnp.int32), axis=1)
    here = own_live[None, :] & (before[None, :] == local[:, None])
    entry = jnp.sum(jnp.where(here, local[None, :], 0), axis=1)
    often = jnp.sum(jnp.where(here, own_times[None, :], 0), axis=1).astype(jnp.float32)
    side = entry // groups
    weights = jnp.stack([jnp.where(side == 0, often, 0.0), jnp.where(side == 1, often, 0.0)])
    return entry % groups, 2 * group + side, weights, most


def on_device(orbitals, exchange_in, window_slot, task_pairs, task_count):
    band_dev, slab_rows, span, _ = orbitals.shape
    grid_parts = lax.axis_size("grid")
    groups = lax.axis_size("band")
    members = 2 * grid_parts
    own_rows = span // members
    band = lax.axis_index("band")
    core, group = band % 2, band // 2
    window, lists = gather_window((4, 4), span, orbitals, window_slot, task_pairs, task_count)
    sources, targets, weights, most = task_lists(lists, task_pairs.shape[-1], groups, group)

    window = window.reshape(groups, -1, LANES)
    member = 2 * lax.axis_index("grid") + core
    constants = (
        quarter_kernel(span, member % QUAD), jnp.asarray(undo_emphasis(span)), jnp.asarray(lane_table(span)),
        jnp.asarray(row_tables(span)),
    )

    def few():
        return run_tasks(3, span, members, sources, targets, weights, window, *constants)

    def many():
        def step(carry):
            start, total = carry
            lists = [lax.dynamic_slice_in_dim(a, start, 16, a.ndim - 1) for a in (sources, targets, weights)]
            return start + 16, total + run_tasks(4, span, members, *lists, window, *constants)

        zero = jnp.zeros((2, own_rows * span, LANES), jnp.float32)
        return lax.while_loop(lambda carry: carry[0] < most, step, (jnp.int32(0), zero))[1]

    owned = lax.cond(most <= 12, few, many)
    owned = owned.reshape(slab_rows, span, LANES)[:, :, :span]
    slot_ids = jnp.arange(band_dev, dtype=jnp.int32)[:, None, None, None]
    return exchange_in + jnp.where(slot_ids == window_slot[0], owned, 0.0)


def solution(mesh):
    in_specs = (
        P("band", "grid", None, None),
        P("band", "grid", None, None),
        P("band"),
        P("band", None, None),
        P("band"),
    )
    out_specs = P("band", "grid", None, None)
    return jax.shard_map(
        on_device, mesh=mesh, in_specs=in_specs, out_specs=out_specs, check_vma=False
    )
```

```python
import functools
import math

import jax
import jax.numpy as jnp
import numpy as np
from jax import lax
from jax.experimental import pallas as pl
from jax.experimental.pallas import tpu as pltpu
from jax.sharding import PartitionSpec as P

MESH = pl.DeviceIdType.MESH
LANES = 128
QUAD = 4
UNROLL = 3


def hartley_table(length):
    steps_all = np.arange(length)
    angle = (steps_all[:, None] * steps_all[None, :] % length) * (2.0 * math.pi / length)
    return np.cos(angle) + np.sin(angle)


def split_table(length):
    table = hartley_table(length).astype(np.float32)
    high = table.astype(jnp.bfloat16)
    low = (table - high.astype(np.float32)).astype(jnp.bfloat16)
    return high, low


def lane_table(length):
    high, low = split_table(length)
    out = np.zeros((2 * LANES, 2 * LANES), jnp.bfloat16)
    out[:length, :length] = high
    out[:length, LANES : LANES + length] = low
    out[LANES : LANES + length, :length] = high
    return out


def row_tables(length):
    high, low = split_table(length)
    order = np.concatenate([np.arange(0, length, 2), np.arange(1, length, 2)])
    out = np.zeros((3, 2 * length, 2 * length), jnp.bfloat16)
    plain = np.arange(length)
    for which, pick in enumerate((np.ix_(plain, plain), np.ix_(plain, order), np.ix_(order, plain))):
        out[which, :length, :length] = high[pick]
        out[which, :length, length:] = high[pick]
        out[which, length:, :length] = low[pick]
    return out


def emphasis(length):
    steps_all = np.arange(length)
    signed = np.where(steps_all <= length // 2, steps_all, steps_all - length).astype(np.float64)
    return ((signed**2)[:, None] + (signed**2)[None, :] + 1.0) ** 0.75


def undo_emphasis(length):
    out = np.zeros((length, LANES), np.float32)
    out[:, :length] = 1.0 / emphasis(length)
    return out


def quarter_kernels(span):
    steps_all = np.arange(span)
    wave = np.where(steps_all <= span // 2, steps_all, steps_all - span) * (2.0 * math.pi / span)
    square = (wave**2)[:, None, None] + (wave**2)[None, :, None] + (wave**2)[None, None, :]
    safe = np.where(square > 0, square, 1.0)
    kernel = np.where(square > 0, 4.0 * math.pi / span**3 / safe, 0.0) * emphasis(span)
    kernel = np.pad(kernel, ((0, 0), (0, 0), (0, LANES - span))).reshape(span, QUAD, span // QUAD, LANES)
    return kernel.transpose(1, 0, 2, 3).reshape(QUAD, -1, LANES).astype(np.float32)


def split(values):
    high = values.astype(jnp.bfloat16)
    return high, (values - high.astype(jnp.float32)).astype(jnp.bfloat16)


def unpack(values):
    rows = values.shape[0] // 3
    parts = [values[third * rows : (third + 1) * rows] for third in range(3)]
    lane = lax.broadcasted_iota(jnp.int32, (rows, LANES), 1)
    turned = [pltpu.roll(parts[third], 32 * (third + 1), 1) for third in range(3)]
    last = jnp.where(lane < 32, turned[0], jnp.where(lane < 64, turned[1], turned[2]))
    return jnp.concatenate([jnp.where(lane < 96, part, 0.0) for part in (*parts, last)], axis=0)


LEVELS = 32766.0
FINE = 2.0**24
STEPS = 256.0
LN2 = math.log(2.0)


def grade(peak):
    return jnp.ceil(jnp.log(jnp.maximum(peak, 1e-30)) * (STEPS / LN2) + 0.01)


def size(graded):
    return jnp.exp(graded * (LN2 / STEPS))


def nearest(values):
    return jnp.round(values).astype(jnp.int32)


def encode(first, second):
    lane = lax.broadcasted_iota(jnp.int32, first.shape, 1)
    top = grade(jnp.max(jnp.maximum(jnp.abs(first), jnp.abs(second)), axis=(0, 1), keepdims=True))
    factor = LEVELS / size(top)
    word = nearest(first * factor) * 65536 + nearest(second * factor)
    return jnp.where(lane == 96, top.astype(jnp.int32), word)


def encode_apart(first, second):
    lane = lax.broadcasted_iota(jnp.int32, (1, LANES), 1)
    peaks = jnp.max(jnp.maximum(jnp.abs(first), jnp.abs(second)), axis=0, keepdims=True)
    top = grade(jnp.max(jnp.where(lane > 0, peaks, 0.0), axis=1, keepdims=True))
    high = grade(jnp.max(jnp.where(lane > 0, 0.0, peaks), axis=1, keepdims=True))
    factor = jnp.where(lane > 0, LEVELS / size(top), FINE / size(high))
    first, second = nearest(first * factor), nearest(second * factor)
    lane = lax.broadcasted_iota(jnp.int32, first.shape, 1)
    word = jnp.where(lane > 0, first * 65536 + second, first)
    word = jnp.where(lane == 96, pltpu.roll(second, 96, 1), word)
    return jnp.where(lane == 97, top.astype(jnp.int32), jnp.where(lane == 98, high.astype(jnp.int32), word))


def halves(word):
    second = lax.shift_right_arithmetic(lax.shift_left(word, 16), 16)
    return lax.shift_right_arithmetic(word - second, 16), second


def scale_of(word):
    return size(word[:, 96:97].astype(jnp.float32)) * (1.0 / LEVELS)


def decode(word, scale):
    return [half.astype(jnp.float32) * scale for half in halves(word)]


def scale_apart(word):
    lane = lax.broadcasted_iota(jnp.int32, word.shape, 1)
    rest = size(word[:, 97:98].astype(jnp.float32)) * (1.0 / LEVELS)
    return jnp.where(lane > 0, rest, size(word[:, 98:99].astype(jnp.float32)) * (1.0 / FINE))


def decode_apart(word, scale):
    lane = lax.broadcasted_iota(jnp.int32, word.shape, 1)
    first, second = halves(word)
    first, second = jnp.where(lane > 0, first, word), jnp.where(lane > 0, second, pltpu.roll(word, 32, 1))
    return [first.astype(jnp.float32) * scale, second.astype(jnp.float32) * scale]


def along_lanes(values, table):
    both = jnp.dot(jnp.concatenate(split(values), axis=1), table, preferred_element_type=jnp.float32)
    return both[:, :LANES] + both[:, LANES:]


def along_rows(values, table):
    both = jnp.dot(table, jnp.concatenate(split(values), axis=0), preferred_element_type=jnp.float32)
    span = values.shape[0]
    return both[:span] + both[span:]


def task_kernel(
    quads, span, start_ref, list_ref, window_ref, kernels_ref, undo_ref, lane_ref, row_ref, out_ref,
    kernel_ref, send_out, recv_out, send_back, recv_back, total, partner_part,
    out_send_sem, out_recv_sem, back_send_sem, back_recv_sem, part_sems, kernel_sem,
):
    band = lax.axis_index("band")
    core = lax.rem(band, 2)
    pair = band - core
    members = 2 * lax.axis_size("grid")
    me = 2 * lax.axis_index("grid") + core
    own_rows = span // members
    rows = span // QUAD
    block = own_rows // 2 * rows

    def place(member):
        return {"band": pair + lax.rem(member, 2), "grid": member // 2}

    kernel_copy = pltpu.make_async_copy(kernels_ref.at[lax.rem(me, QUAD)], kernel_ref, kernel_sem.at[0])
    kernel_copy.start()
    barrier = pltpu.get_barrier_semaphore()

    def greet(step, carry):
        pl.semaphore_signal(barrier, inc=1, device_id=place(lax.rem(me + step, members)), device_id_type=MESH)
        return carry

    lax.fori_loop(1, members, greet, 0)

    def at(ref, quad, member):
        return ref.at[quad, pl.ds(pl.multiple_of(member * block, 8), block)]

    def remote(quad, member, origin, src, dst, send_sem, recv_sem):
        return pltpu.make_async_remote_copy(
            src_ref=at(src, quad, member), dst_ref=at(dst, quad, origin),
            send_sem=send_sem.at[quad, member], recv_sem=recv_sem.at[quad, origin],
            device_id=place(member), device_id_type=MESH,
        )

    def local(quad, src, dst, recv_sem):
        return pltpu.make_async_copy(at(src, quad, me), at(dst, quad, me), recv_sem.at[quad, me])

    def start_all(quad, src, dst, send_sem, recv_sem):
        def step_one(step, carry):
            remote(quad, lax.rem(me + step, members), me, src, dst, send_sem, recv_sem).start()
            return carry

        lax.fori_loop(1, members, step_one, 0)
        local(quad, src, dst, recv_sem).start()

    def wait_recv(quad, src, dst, send_sem, recv_sem):
        def step_one(step, carry):
            other = lax.rem(me + step, members)
            remote(quad, other, other, src, dst, send_sem, recv_sem).wait_recv()
            return carry

        lax.fori_loop(1, members, step_one, 0)
        local(quad, src, dst, recv_sem).wait()

    def wait_send(quad, src, dst, send_sem, recv_sem):
        def step_one(step, carry):
            other = lax.rem(me + step, members)
            remote(quad, other, me, src, dst, send_sem, recv_sem).wait_send()
            return carry

        lax.fori_loop(1, members, step_one, 0)

    outward = (send_out, recv_out, out_send_sem, out_recv_sem)
    backward = (send_back, recv_back, back_send_sem, back_recv_sem)

    packed = window_ref.shape[1] // (own_rows // 2)

    def window_part(position, two):
        return window_ref[position, pl.ds(two * packed, packed)].astype(jnp.float32)

    def task(quad, slot):
        index = start_ref[0] + quad * QUAD + slot
        entry = list_ref[0, index]
        groups = lax.axis_size("band")
        return lax.rem(entry, groups), entry // groups, list_ref[1, index].astype(jnp.float32)

    def inner(quad):
        def one(slot, carry):
            source, side, _ = task(quad, slot)
            target = pair + side
            for two in range(own_rows // 2):
                density = window_part(source, two) * window_part(target, two)
                mixed = along_lanes(unpack(density), lane_ref[...])
                mixed = along_rows(jnp.concatenate([mixed[:span], mixed[span:]], axis=1), row_ref[0])
                word = encode_apart(mixed[:, :LANES], mixed[:, LANES:])
                for quarter in range(QUAD):
                    start = (slot * QUAD + quarter) * block + two * rows
                    send_out[quad, pl.ds(pl.multiple_of(start, 8), rows)] = word[quarter * rows : (quarter + 1) * rows]
            return carry

        lax.fori_loop(0, QUAD, one, 0)

    def outer(quad):
        wait_recv(quad, *outward)
        scale = scale_apart(recv_out[quad, pl.ds(0, span // 2, stride=rows)])

        def some(step, carry):
            pairs = [step * UNROLL + i for i in range(UNROLL)]
            picks = [[pl.ds(2 * two + half, span // 2, stride=rows) for half in range(2)] for two in pairs]
            words = [[recv_out[quad, pick] for pick in both] for both in picks]
            values = [
                jnp.concatenate([jnp.concatenate(decode_apart(word, scale), axis=0) for word in both], axis=1)
                for both in words
            ]
            mixed = [along_rows(value, row_ref[1]) for value in values]
            factors = [
                jnp.concatenate([kernel_ref[pl.ds(2 * two + half, span, stride=rows)] for half in range(2)], axis=1)
                for two in pairs
            ]
            restored = [along_rows(value * factor, row_ref[2]) for value, factor in zip(mixed, factors)]
            sides = [slice(half * LANES, (half + 1) * LANES) for half in range(2)]
            words = [[encode(value[: span // 2, side], value[span // 2 :, side]) for side in sides] for value in restored]
            for both, pair_words in zip(picks, words):
                for pick, word in zip(both, pair_words):
                    send_back[quad, pick] = word
            return carry

        lax.fori_loop(0, rows // 2 // UNROLL, some, 0)
        start_all(quad, *backward)

    def finish(quad):
        wait_recv(quad, *backward)

        def one(slot, carry):
            source, wanted, often = task(quad, slot)
            weights = [jnp.where(wanted == side, often, 0.0) for side in range(2)]

            def arrived(two):
                starts = [(slot * QUAD + quarter) * block + two * rows for quarter in range(QUAD)]
                return jnp.concatenate(
                    [recv_back[quad, pl.ds(pl.multiple_of(start, 8), rows)] for start in starts], axis=0
                )

            scale = scale_of(arrived(0)) * undo_ref[...]
            for two in range(own_rows // 2):
                mixed = decode(arrived(two), scale)
                mixed = along_rows(jnp.concatenate(mixed, axis=1), row_ref[0])
                potential = along_lanes(
                    jnp.concatenate([mixed[:, :LANES], mixed[:, LANES:]], axis=0), lane_ref[...]
                )
                part = pl.ds(2 * two * span, 2 * span)
                action = potential * unpack(window_part(source, two))
                for side in range(2):
                    total[side, part] += action * weights[side]
            return carry

        lax.fori_loop(0, QUAD, one, 0)

    total[...] = jnp.zeros_like(total)
    for quad in range(quads):
        inner(quad)
        if quad == 0:
            pl.semaphore_wait(barrier, members - 1)
        start_all(quad, *outward)
    kernel_copy.wait()
    for quad in range(quads):
        outer(quad)
        if quad > 0:
            finish(quad - 1)
    finish(quads - 1)

    swap = pltpu.make_async_remote_copy(
        src_ref=total.at[1 - core], dst_ref=partner_part, send_sem=part_sems.at[0], recv_sem=part_sems.at[1],
        device_id={"band": pair + 1 - core, "grid": lax.axis_index("grid")}, device_id_type=MESH,
    )
    swap.start()
    out_ref[core] = total[core]
    swap.wait_recv()
    out_ref[1 - core] = partner_part[...]
    swap.wait_send()
    for quad in range(quads):
        wait_send(quad, *outward)
        wait_send(quad, *backward)


def run_tasks(quads, span, members, *operands):
    own_rows = span // members
    whole = (quads, span * span // QUAD // 2, LANES)
    smem, vmem = pl.BlockSpec(memory_space=pltpu.SMEM), pl.BlockSpec(memory_space=pltpu.VMEM)
    sems = pltpu.SemaphoreType.DMA((quads, members))
    return pl.pallas_call(
        functools.partial(task_kernel, quads, span),
        out_shape=jax.ShapeDtypeStruct((2, own_rows * span, LANES), jnp.float32),
        in_specs=[smem] * 2 + [vmem] + [pl.BlockSpec(memory_space=pl.ANY)] + [vmem] * 3,
        out_specs=vmem,
        scratch_shapes=[pltpu.VMEM((span * span // QUAD, LANES), jnp.float32)]
        + [pltpu.VMEM(whole, jnp.int32)] * 4
        + [pltpu.VMEM((2, own_rows * span, LANES), jnp.float32), pltpu.VMEM((own_rows * span, LANES), jnp.float32)]
        + [sems] * 4
        + [pltpu.SemaphoreType.DMA((2,)), pltpu.SemaphoreType.DMA((1,))],
        compiler_params=pltpu.CompilerParams(
            collective_id=quads, has_side_effects=True, vmem_limit_bytes=56 * 1024 * 1024
        ),
        name="exchange_tasks",
    )(*operands)


def distinct_tasks(lists_ref, cap, chip):
    groups = lists_ref.shape[0]
    span = 2 * groups
    lane = lax.broadcasted_iota(jnp.int32, (groups, LANES), 1)
    live = lane < jnp.minimum(lists_ref[:, 2, :], cap)
    key = jnp.where(live, lists_ref[:, 1, :] * groups + lists_ref[:, 0, :], -1)
    per_row = LANES // span
    row_lane = lax.broadcasted_iota(jnp.int32, (1, LANES), 1)
    own = jnp.zeros((1, LANES), jnp.float32)
    most = jnp.zeros((1, 1), jnp.float32)
    for chunk in range(groups * groups // LANES):
        times = jnp.zeros((groups, LANES), jnp.float32)
        for slot in range(cap):
            times += jnp.where(key[:, slot : slot + 1] == lane + chunk * LANES, 1.0, 0.0)
        times = jnp.sum(times, axis=0, keepdims=True)
        for place in range(per_row):
            inside = (row_lane >= place * span) & (row_lane < (place + 1) * span)
            count = jnp.sum(jnp.where(inside & (times > 0.0), 1.0, 0.0), axis=1, keepdims=True)
            most = jnp.maximum(most, count)
            turned = pltpu.roll(times, (LANES - place * span) % LANES, 1) if place else times
            own += jnp.where((chip == chunk * per_row + place) & (row_lane < span), turned, 0.0)
    shape = (LANES, LANES)
    down, across = lax.broadcasted_iota(jnp.int32, shape, 0), lax.broadcasted_iota(jnp.int32, shape, 1)
    own_down = jnp.sum(jnp.where(down == across, own, 0.0), axis=1, keepdims=True)
    before = jnp.sum(jnp.where((across < down) & (own > 0.0), 1.0, 0.0), axis=1, keepdims=True)
    here = (before == across.astype(jnp.float32)) & (own_down > 0.0)
    entry = jnp.sum(jnp.where(here, down.astype(jnp.float32), 0.0), axis=0, keepdims=True)
    often = jnp.sum(jnp.where(here, own_down, 0.0), axis=0, keepdims=True)
    row = lax.broadcasted_iota(jnp.int32, (8, LANES), 0)
    return jnp.where(row == 0, entry, jnp.where(row == 1, often, most)).astype(jnp.int32)


def gather_kernel(
    rings, span, orbital_ref, slot_ref, pairs_ref, count_ref, window_ref, list_ref, lists_ref, give, own_list,
    swap_sems, list_send, list_recv, near_send, near_recv, far_send, far_recv,
):
    ring_x, ring_z = rings
    band = lax.axis_index("band")
    groups = lax.axis_size("band")
    core, chip = lax.rem(band, 2), band // 2
    at_x, at_z = chip // ring_z, lax.rem(chip, ring_z)
    packed = window_ref.shape[0] // groups

    barrier = pltpu.get_barrier_semaphore()

    def greet(step, carry):
        pl.semaphore_signal(barrier, inc=1, device_id={"band": lax.rem(band + step, groups)}, device_id_type=MESH)
        return carry

    lax.fori_loop(1, groups, greet, 0)

    part_rows = packed // 3
    quarter = part_rows // 3
    first = slot_ref[0] == 0
    for two in range(3):
        for side in range(2):
            rows = pl.ds(side * (orbital_ref.shape[1] // 2) + two * 4 * quarter, 4 * quarter)
            values = jnp.where(
                first, orbital_ref[0, rows].astype(jnp.float32), orbital_ref[1, rows].astype(jnp.float32)
            )
            last = values[3 * quarter :]
            for third in range(3):
                full = jnp.concatenate(
                    [values[third * quarter : (third + 1) * quarter], last[:, 32 * third : 32 * third + 32]], axis=1
                ).astype(jnp.bfloat16)
                row = two * part_rows + third * quarter

                @pl.when(core == side)
                def _():
                    window_ref[pl.ds(pl.multiple_of(band * packed + row, 16), quarter)] = full

                @pl.when(core != side)
                def _():
                    give[pl.ds(row, quarter)] = full

    own_list[...] = jnp.zeros_like(own_list)
    own_list[0:2, 0 : pairs_ref.shape[1]] = pairs_ref[...]
    own_list[2:3] = jnp.full((1, LANES), count_ref[0], jnp.int32)

    pl.semaphore_wait(barrier, groups - 1)

    def blocks(first_band, count):
        return window_ref.at[pl.ds(pl.multiple_of(first_band * packed, 16), count * packed)]

    def send(src, dst, send_sem, recv_sem, target):
        return pltpu.make_async_remote_copy(
            src_ref=src, dst_ref=dst, send_sem=send_sem, recv_sem=recv_sem,
            device_id={"band": target}, device_id_type=MESH,
        )

    def swap(owner):
        return send(give, blocks(owner, 1), swap_sems.at[0], swap_sems.at[1], band + 1 - 2 * core)

    swap(band).start()

    def send_list(step, owner):
        other = lax.rem(band + step, groups)
        return send(own_list, lists_ref.at[owner], list_send.at[step], list_recv.at[step], other)

    def start_list(step, carry):
        send_list(step, band).start()
        return carry

    def place(x, z):
        return lax.rem(x + ring_x, ring_x) * ring_z + lax.rem(z + ring_z, ring_z)

    level = (0, -1, 1, 2)
    later = packed // 9
    main, rest = (1, 0, 0, packed - later), (0, 1, packed - later, later)
    number = {main: 0, rest: 1}

    def along(plan, ring, step):
        move = [0, 0]
        if ring == 0:
            move[plan[0]] = step
        else:
            move[plan[1]], move[plan[0]] = step, level[ring - 1]
        return place(at_x + move[0], at_z + move[1])

    def neighbour(plan, ring, step):
        move = [0, 0]
        move[plan[min(ring, 1)]] = step
        return 2 * place(at_x + move[0], at_z + move[1]) + core

    def piece(plan, chip_at, half):
        return window_ref.at[pl.ds(pl.multiple_of((2 * chip_at + half) * packed + plan[2], 16), plan[3])]

    def near(plan, ring, way, half):
        block = piece(plan, along(plan, ring, 0), half)
        sems = [sem.at[number[plan], ring, way, half] for sem in (near_send, near_recv)]
        return send(block, block, *sems, neighbour(plan, ring, 1 - 2 * way))

    def far(plan, ring, way):
        block = piece(plan, along(plan, ring, -1 + 2 * way), way)
        sems = [sem.at[number[plan], ring, way] for sem in (far_send, far_recv)]
        return send(block, block, *sems, neighbour(plan, ring, 1 - 2 * way))

    def begin_half(plan, ring, half):
        for way in range(2):
            near(plan, ring, way, half).start()

    def begin(plan, ring):
        for turn in range(2):
            for way in range(2):
                near(plan, ring, way, way if turn == 0 else 1 - way).start()

    def onward(plan, ring, way):
        near(plan, ring, way, way).wait_recv()
        far(plan, ring, way).start()

    swap(band).wait_recv()
    begin(main, 0)
    begin(main, 1)
    begin(rest, 0)
    lax.fori_loop(1, groups, start_list, 0)
    for way in range(2):
        onward(main, 0, way)
        begin_half(main, 2 + way, way)
    for way in range(2):
        onward(rest, 0, way)
        onward(main, 1, way)
    for way in range(2):
        near(main, 0, way, 1 - way).wait_recv()
        begin_half(main, 2 + way, 1 - way)
    for way in range(2):
        far(main, 0, way).wait_recv()
        begin_half(main, 4, way)
    begin(rest, 1)
    for way in range(2):
        near(rest, 0, way, 1 - way).wait_recv()
        begin(rest, 2 + way)
    for turn in range(2):
        for way in range(2):
            onward(main, 2 + way, way if turn == 0 else 1 - way)
    for way in range(2):
        far(rest, 0, way).wait_recv()
    begin(rest, 4)
    for ring in range(1, 4):
        for way in range(2):
            onward(rest, ring, way)

    def end_list(step, carry):
        send_list(step, band).wait_recv()
        send_list(step, band).wait_send()
        return carry

    lax.fori_loop(1, groups, end_list, 0)
    lists_ref[band] = own_list[...]
    list_ref[...] = distinct_tasks(lists_ref, pairs_ref.shape[1], chip)

    for plan in (main, rest):
        for way in range(2):
            onward(plan, 4, way)
    for plan in (main, rest):
        for ring in range(1, 5):
            for way in range(2):
                near(plan, ring, way, 1 - way).wait_recv()
                far(plan, ring, way).wait_recv()
    swap(band).wait_send()
    for plan in (main, rest):
        for ring in range(5):
            for way in range(2):
                near(plan, ring, way, 0).wait_send()
                near(plan, ring, way, 1).wait_send()
                far(plan, ring, way).wait_send()


def gather_window(rings, span, orbitals, window_slot, task_pairs, task_count):
    groups = lax.axis_size("band")
    slab_rows = orbitals.shape[1]
    packed = slab_rows // 2 * span * span // LANES
    smem, vmem = pl.BlockSpec(memory_space=pltpu.SMEM), pl.BlockSpec(memory_space=pltpu.VMEM)
    dma = pltpu.SemaphoreType.DMA
    return pl.pallas_call(
        functools.partial(gather_kernel, rings, span),
        out_shape=(
            jax.ShapeDtypeStruct((groups * packed, LANES), jnp.bfloat16),
            jax.ShapeDtypeStruct((8, LANES), jnp.int32),
        ),
        in_specs=[vmem, smem, vmem, smem],
        out_specs=(vmem, vmem),
        scratch_shapes=[pltpu.VMEM((groups, 8, LANES), jnp.int32)]
        + [pltpu.VMEM((packed, LANES), jnp.bfloat16), pltpu.VMEM((8, LANES), jnp.int32)]
        + [dma((2,)), dma((groups,)), dma((groups,))]
        + [dma((2, 5, 2, 2))] * 2
        + [dma((2, 5, 2))] * 2,
        compiler_params=pltpu.CompilerParams(
            collective_id=9, has_side_effects=True, vmem_limit_bytes=56 * 1024 * 1024
        ),
        name="gather_window",
    )(orbitals.reshape(2, slab_rows * span, span), window_slot, task_pairs[0], task_count)


def on_device(orbitals, exchange_in, window_slot, task_pairs, task_count):
    band_dev, slab_rows, span, _ = orbitals.shape
    grid_parts = lax.axis_size("grid")
    groups = lax.axis_size("band")
    members = 2 * grid_parts
    own_rows = span // members
    window, lists = gather_window((4, 4), span, orbitals, window_slot, task_pairs, task_count)
    window = window.reshape(groups, -1, LANES)
    constants = [jnp.asarray(a) for a in (quarter_kernels(span), undo_emphasis(span), lane_table(span), row_tables(span))]
    most = lists[2, 0]

    def few():
        return run_tasks(3, span, members, jnp.zeros((1,), jnp.int32), lists, window, *constants)

    def many():
        def step(carry):
            start, total = carry
            return start + 16, total + run_tasks(4, span, members, start[None], lists, window, *constants)

        zero = jnp.zeros((2, own_rows * span, LANES), jnp.float32)
        return lax.while_loop(lambda carry: carry[0] < most, step, (jnp.int32(0), zero))[1]

    owned = lax.cond(most <= 12, few, many)
    owned = owned.reshape(slab_rows, span, LANES)[:, :, :span]
    slot_ids = jnp.arange(band_dev, dtype=jnp.int32)[:, None, None, None]
    return exchange_in + jnp.where(slot_ids == window_slot[0], owned, 0.0)


def solution(mesh):
    in_specs = (
        P("band", "grid", None, None),
        P("band", "grid", None, None),
        P("band"),
        P("band", None, None),
        P("band"),
    )
    out_specs = P("band", "grid", None, None)
    return jax.shard_map(
        on_device, mesh=mesh, in_specs=in_specs, out_specs=out_specs, check_vma=False
    )
```

```python
import functools
import math

import jax
import jax.numpy as jnp
import numpy as np
from jax import lax
from jax.experimental import pallas as pl
from jax.experimental.pallas import tpu as pltpu
from jax.sharding import PartitionSpec as P

MESH = pl.DeviceIdType.MESH
LANES = 128
QUAD = 4


def hartley_table(length):
    steps_all = np.arange(length)
    angle = (steps_all[:, None] * steps_all[None, :] % length) * (2.0 * math.pi / length)
    return np.cos(angle) + np.sin(angle)


def split_table(length):
    table = hartley_table(length).astype(np.float32)
    high = table.astype(jnp.bfloat16)
    low = (table - high.astype(np.float32)).astype(jnp.bfloat16)
    return high, low


def lane_table(length):
    high, low = split_table(length)
    out = np.zeros((2 * LANES, 2 * LANES), jnp.bfloat16)
    out[:length, :length] = high
    out[:length, LANES : LANES + length] = low
    out[LANES : LANES + length, :length] = high
    return out


def row_tables(length):
    high, low = split_table(length)
    order = np.arange(length).reshape(-1, 3, 2).transpose(2, 1, 0).reshape(-1)
    out = np.zeros((3, 2 * length, 2 * length), jnp.bfloat16)
    plain = np.arange(length)
    for which, pick in enumerate((np.ix_(plain, plain), np.ix_(plain, order), np.ix_(order, plain))):
        out[which, :length, :length] = high[pick]
        out[which, :length, length:] = high[pick]
        out[which, length:, :length] = low[pick]
    return out


def emphasis(length):
    steps_all = np.arange(length)
    signed = np.where(steps_all <= length // 2, steps_all, steps_all - length).astype(np.float64)
    return ((signed**2)[:, None] + (signed**2)[None, :] + 1.0) ** 0.75


def undo_emphasis(length):
    out = np.zeros((length, LANES), np.float32)
    out[:, :length] = 1.0 / emphasis(length)
    return out


def quarter_kernels(span):
    steps_all = np.arange(span)
    wave = np.where(steps_all <= span // 2, steps_all, steps_all - span) * (2.0 * math.pi / span)
    square = (wave**2)[:, None, None] + (wave**2)[None, :, None] + (wave**2)[None, None, :]
    safe = np.where(square > 0, square, 1.0)
    kernel = np.where(square > 0, 4.0 * math.pi / span**3 / safe, 0.0) * emphasis(span)
    kernel = np.pad(kernel, ((0, 0), (0, 0), (0, LANES - span))).reshape(span, QUAD, span // QUAD, LANES)
    return kernel.transpose(1, 0, 2, 3).reshape(QUAD, -1, LANES).astype(np.float32)


def split(values):
    high = values.astype(jnp.bfloat16)
    return high, (values - high.astype(jnp.float32)).astype(jnp.bfloat16)


def unpack(values):
    rows = values.shape[0] // 3
    parts = [values[third * rows : (third + 1) * rows] for third in range(3)]
    lane = lax.broadcasted_iota(jnp.int32, (rows, LANES), 1)
    turned = [pltpu.roll(parts[third], 32 * (third + 1), 1) for third in range(3)]
    last = jnp.where(lane < 32, turned[0], jnp.where(lane < 64, turned[1], turned[2]))
    return jnp.concatenate([jnp.where(lane < 96, part, 0.0) for part in (*parts, last)], axis=0)


LEVELS = 32766.0
FINE = 2.0**24
STEPS = 256.0
LN2 = math.log(2.0)


def grade(peak):
    return jnp.ceil(jnp.log(jnp.maximum(peak, 1e-30)) * (STEPS / LN2) + 0.01)


def size(graded):
    return jnp.exp(graded * (LN2 / STEPS))


def nearest(values):
    return jnp.round(values).astype(jnp.int32)


def lanes_of(values):
    return lax.broadcasted_iota(jnp.int32, values.shape, 1)


def encode(first, second):
    top = grade(jnp.max(jnp.maximum(jnp.abs(first), jnp.abs(second)), axis=(0, 1), keepdims=True))
    factor = LEVELS / size(top)
    return nearest(first * factor) * 65536 + nearest(second * factor), top.astype(jnp.int32)


def encode_apart(first, second):
    lane = lax.broadcasted_iota(jnp.int32, (1, LANES), 1)
    peaks = jnp.max(jnp.maximum(jnp.abs(first), jnp.abs(second)), axis=0, keepdims=True)
    top = grade(jnp.max(jnp.where(lane > 0, peaks, 0.0), axis=1, keepdims=True))
    high = grade(jnp.max(jnp.where(lane > 0, 0.0, peaks), axis=1, keepdims=True))
    factor = jnp.where(lane > 0, LEVELS / size(top), FINE / size(high))
    first, second = nearest(first * factor), nearest(second * factor)
    word = jnp.where(lanes_of(first) > 0, first * 65536 + second, first)
    return word, second, top.astype(jnp.int32), high.astype(jnp.int32)


def halves(word):
    second = lax.shift_right_arithmetic(lax.shift_left(word, 16), 16)
    return lax.shift_right_arithmetic(word - second, 16), second


def decode(word, scale):
    return [half.astype(jnp.float32) * scale for half in halves(word)]


def decode_apart(word, second_apart, scale):
    lane = lanes_of(word)
    first, second = halves(word)
    first, second = jnp.where(lane > 0, first, word), jnp.where(lane > 0, second, second_apart)
    return [first.astype(jnp.float32) * scale, second.astype(jnp.float32) * scale]


def beside(full, third, turn):
    return jnp.where(lanes_of(full) < 96, full, pltpu.roll(third, turn, 1))


def tail_lanes(pieces):
    lane = lanes_of(pieces[0])
    first, second = pltpu.roll(pieces[0], 64, 1), pltpu.roll(pieces[1], 96, 1)
    return jnp.where(lane < 32, first, jnp.where(lane < 64, second, pieces[2]))


def third_of(full, second_full, tail, group):
    lane = lanes_of(full)
    last = pltpu.roll(tail, 64 - 32 * group, 1) if group < 2 else tail
    return jnp.where(lane < 32, pltpu.roll(full, 32, 1), jnp.where(lane < 64, pltpu.roll(second_full, 64, 1), last))


def put(values, lane_at, column):
    return jnp.where(lanes_of(values) == lane_at, column, values)


def along_lanes(values, table):
    both = jnp.dot(jnp.concatenate(split(values), axis=1), table, preferred_element_type=jnp.float32)
    return both[:, :LANES] + both[:, LANES:]


def along_rows(values, table):
    both = jnp.dot(table, jnp.concatenate(split(values), axis=0), preferred_element_type=jnp.float32)
    span = values.shape[0]
    return both[:span] + both[span:]


def task_kernel(
    quads, span, start_ref, list_ref, window_ref, kernels_ref, undo_ref, lane_ref, row_ref, out_ref,
    kernel_ref, send_out, recv_out, send_back, recv_back, total, partner_part,
    out_send_sem, out_recv_sem, back_send_sem, back_recv_sem, part_sems, kernel_sem,
):
    band = lax.axis_index("band")
    core = lax.rem(band, 2)
    pair = band - core
    members = 2 * lax.axis_size("grid")
    me = 2 * lax.axis_index("grid") + core
    own_rows = span // members
    rows = span // QUAD
    block = 2 * rows + rows // 3
    eighth = rows // 3
    my_slot = me // QUAD

    def place(member):
        return {"band": pair + lax.rem(member, 2), "grid": member // 2}

    kernel_copy = pltpu.make_async_copy(kernels_ref.at[lax.rem(me, QUAD)], kernel_ref, kernel_sem.at[0])
    kernel_copy.start()
    barrier = pltpu.get_barrier_semaphore()

    def greet(step, carry):
        pl.semaphore_signal(barrier, inc=1, device_id=place(lax.rem(me + step, members)), device_id_type=MESH)
        return carry

    lax.fori_loop(1, members, greet, 0)

    def at(ref, quad, member):
        return ref.at[quad, pl.ds(pl.multiple_of(member * block, 8), block)]

    def remote(quad, member, origin, src, dst, send_sem, recv_sem):
        return pltpu.make_async_remote_copy(
            src_ref=at(src, quad, member), dst_ref=at(dst, quad, origin),
            send_sem=send_sem.at[quad, member], recv_sem=recv_sem.at[quad, origin],
            device_id=place(member), device_id_type=MESH,
        )

    def local(quad, src, dst, recv_sem):
        return pltpu.make_async_copy(at(src, quad, me), at(dst, quad, me), recv_sem.at[quad, me])

    def start_one(quad, member, src, dst, send_sem, recv_sem):
        @pl.when(member != me)
        def _():
            remote(quad, member, me, src, dst, send_sem, recv_sem).start()

        @pl.when(member == me)
        def _():
            local(quad, src, dst, recv_sem).start()

    def start_all(quad, *way):
        def step_one(step, carry):
            start_one(quad, lax.rem(me + step, members), *way)
            return carry

        lax.fori_loop(1, members + 1, step_one, 0)

    def wait_one(quad, member, src, dst, send_sem, recv_sem):
        @pl.when(member != me)
        def _():
            remote(quad, member, member, src, dst, send_sem, recv_sem).wait_recv()

        @pl.when(member == me)
        def _():
            local(quad, src, dst, recv_sem).wait()

    def wait_recv(quad, *way):
        def step_one(step, carry):
            wait_one(quad, lax.rem(me + step, members), *way)
            return carry

        lax.fori_loop(1, members + 1, step_one, 0)

    def wait_send(quad, src, dst, send_sem, recv_sem):
        def step_one(step, carry):
            other = lax.rem(me + step, members)
            remote(quad, other, me, src, dst, send_sem, recv_sem).wait_send()
            return carry

        lax.fori_loop(1, members, step_one, 0)

    outward = (send_out, recv_out, out_send_sem, out_recv_sem)
    backward = (send_back, recv_back, back_send_sem, back_recv_sem)

    packed = window_ref.shape[1] // (own_rows // 2)

    def window_part(position, two):
        return window_ref[position, pl.ds(two * packed, packed)].astype(jnp.float32)

    def task(quad, slot):
        index = start_ref[0] + quad * QUAD + slot
        entry = list_ref[0, index]
        groups = lax.axis_size("band")
        return lax.rem(entry, groups), entry // groups, list_ref[1, index].astype(jnp.float32)

    def inner(quad):
        def one(step, carry):
            slot = lax.rem(my_slot + 1 + step, QUAD)
            source, side, _ = task(quad, slot)
            target = pair + side
            parts = range(own_rows // 2)
            mixed = [along_lanes(unpack(window_part(source, two) * window_part(target, two)), lane_ref[...]) for two in parts]
            mixed = [along_rows(jnp.concatenate([value[:span], value[span:]], axis=1), row_ref[0]) for value in mixed]
            coded = [encode_apart(value[:, :LANES], value[:, LANES:]) for value in mixed]
            words, seconds, tops, highs = zip(*coded)
            for quarter in range(QUAD):
                start = (slot * QUAD + quarter) * block
                here = slice(quarter * rows, (quarter + 1) * rows)
                third = words[2][here]
                groups = [slice(quarter * rows + g * eighth, quarter * rows + (g + 1) * eighth) for g in range(3)]
                tail = tail_lanes([words[2][group] for group in groups])
                for two in parts:
                    for g, group in enumerate(groups):
                        at_lane = 96 + 3 * two + g
                        tail = put(tail, at_lane, pltpu.roll(seconds[two][group], at_lane, 1))
                    tail = put(put(tail, 105 + 2 * two, tops[two]), 106 + 2 * two, highs[two])
                send_out[quad, pl.ds(pl.multiple_of(start, 8), rows)] = beside(words[0][here], third, 96)
                send_out[quad, pl.ds(pl.multiple_of(start + rows, 8), rows)] = beside(words[1][here], third, 64)
                send_out[quad, pl.ds(pl.multiple_of(start + 2 * rows, 8), eighth)] = tail
            for quarter in range(QUAD):
                start_one(quad, slot * QUAD + quarter, *outward)
            return carry

        lax.fori_loop(0, QUAD, one, 0)

    def outer(quad):
        wait_recv(quad, *outward)

        def across(first):
            return pl.ds(first, members, stride=block)

        tail = recv_out[quad, across(2 * rows)]
        scales = []
        for two in range(3):
            rest = size(tail[:, 105 + 2 * two : 106 + 2 * two].astype(jnp.float32)) * (1.0 / LEVELS)
            mean = size(tail[:, 106 + 2 * two : 107 + 2 * two].astype(jnp.float32)) * (1.0 / FINE)
            scales.append(jnp.where(lanes_of(tail) > 0, rest, mean))
        scale = jnp.concatenate(scales, axis=0)

        def some(step, carry):
            tails = [recv_out[quad, across(2 * rows + 2 * step + half)] for half in range(2)]
            values = []
            for g in range(3):
                both = []
                for half in range(2):
                    row = g * eighth + 2 * step + half
                    first, second = recv_out[quad, across(row)], recv_out[quad, across(rows + row)]
                    word = jnp.concatenate([first, second, third_of(first, second, tails[half], g)], axis=0)
                    apart = jnp.concatenate([pltpu.roll(tails[half], 32 - 3 * two - g, 1) for two in range(3)], axis=0)
                    both.append(jnp.concatenate(decode_apart(word, apart, scale), axis=0))
                values.append(jnp.concatenate(both, axis=1))
            mixed = [along_rows(value, row_ref[1]) for value in values]
            factors = [
                jnp.concatenate(
                    [kernel_ref[pl.ds(g * eighth + 2 * step + half, span, stride=rows)] for half in range(2)], axis=1
                )
                for g in range(3)
            ]
            restored = [along_rows(value * factor, row_ref[2]) for value, factor in zip(mixed, factors)]
            for half in range(2):
                side = slice(half * LANES, (half + 1) * LANES)
                words, tops = zip(*[encode(value[: span // 2, side], value[span // 2 :, side]) for value in restored])
                thirds = [word[2 * members :] for word in words]
                tail = tail_lanes(thirds)
                for g in range(3):
                    row = g * eighth + 2 * step + half
                    tail = put(tail, 96 + g, tops[g])
                    send_back[quad, across(row)] = beside(words[g][:members], thirds[g], 96)
                    send_back[quad, across(rows + row)] = beside(words[g][members : 2 * members], thirds[g], 64)
                send_back[quad, across(2 * rows + 2 * step + half)] = tail
            return carry

        lax.fori_loop(0, eighth // 2, some, 0)
        start_all(quad, *backward)

    def finish(quad):
        def one(step, carry):
            slot = lax.rem(my_slot + step, QUAD)
            source, wanted, often = task(quad, slot)
            weights = [jnp.where(wanted == side, often, 0.0) for side in range(2)]
            words, scales = [[], [], []], []
            for quarter in range(QUAD):
                wait_one(quad, slot * QUAD + quarter, *backward)
            for quarter in range(QUAD):
                start = (slot * QUAD + quarter) * block
                first, second = [
                    recv_back[quad, pl.ds(pl.multiple_of(start + two * rows, 8), rows)] for two in range(2)
                ]
                tail = recv_back[quad, pl.ds(pl.multiple_of(start + 2 * rows, 8), eighth)]
                words[0].append(first)
                words[1].append(second)
                for g in range(3):
                    group = slice(g * eighth, (g + 1) * eighth)
                    words[2].append(third_of(first[group], second[group], tail, g))
                    scales.append(tail[:, 96 + g : 97 + g])
            scale = size(jnp.concatenate(scales, axis=0).astype(jnp.float32)) * (1.0 / LEVELS) * undo_ref[...]
            parts = range(own_rows // 2)
            mixed = [jnp.concatenate(decode(jnp.concatenate(words[two], axis=0), scale), axis=1) for two in parts]
            mixed = [along_rows(value, row_ref[0]) for value in mixed]
            potentials = [
                along_lanes(jnp.concatenate([value[:, :LANES], value[:, LANES:]], axis=0), lane_ref[...]) for value in mixed
            ]
            for two in parts:
                part = pl.ds(2 * two * span, 2 * span)
                action = potentials[two] * unpack(window_part(source, two))
                for side in range(2):
                    total[side, part] += action * weights[side]
            return carry

        lax.fori_loop(0, QUAD, one, 0)

    total[...] = jnp.zeros_like(total)
    pl.semaphore_wait(barrier, members - 1)
    for quad in range(quads):
        inner(quad)
    kernel_copy.wait()
    for quad in range(quads):
        outer(quad)
    for quad in range(quads):
        finish(quad)

    swap = pltpu.make_async_remote_copy(
        src_ref=total.at[1 - core], dst_ref=partner_part, send_sem=part_sems.at[0], recv_sem=part_sems.at[1],
        device_id={"band": pair + 1 - core, "grid": lax.axis_index("grid")}, device_id_type=MESH,
    )
    swap.start()
    out_ref[core] = total[core]
    swap.wait_recv()
    out_ref[1 - core] = partner_part[...]
    swap.wait_send()
    for quad in range(quads):
        wait_send(quad, *outward)
        wait_send(quad, *backward)


def run_tasks(quads, span, members, *operands):
    own_rows = span // members
    whole = (quads, members * (span // QUAD) * 7 // 3, LANES)
    smem, vmem = pl.BlockSpec(memory_space=pltpu.SMEM), pl.BlockSpec(memory_space=pltpu.VMEM)
    sems = pltpu.SemaphoreType.DMA((quads, members))
    return pl.pallas_call(
        functools.partial(task_kernel, quads, span),
        out_shape=jax.ShapeDtypeStruct((2, own_rows * span, LANES), jnp.float32),
        in_specs=[smem] * 2 + [vmem] + [pl.BlockSpec(memory_space=pl.ANY)] + [vmem] * 3,
        out_specs=vmem,
        scratch_shapes=[pltpu.VMEM((span * span // QUAD, LANES), jnp.float32)]
        + [pltpu.VMEM(whole, jnp.int32)] * 4
        + [pltpu.VMEM((2, own_rows * span, LANES), jnp.float32), pltpu.VMEM((own_rows * span, LANES), jnp.float32)]
        + [sems] * 4
        + [pltpu.SemaphoreType.DMA((2,)), pltpu.SemaphoreType.DMA((1,))],
        compiler_params=pltpu.CompilerParams(
            collective_id=quads, has_side_effects=True, vmem_limit_bytes=56 * 1024 * 1024
        ),
        name="exchange_tasks",
    )(*operands)


def distinct_tasks(lists_ref, cap, chip):
    groups = lists_ref.shape[0]
    span = 2 * groups
    lane = lax.broadcasted_iota(jnp.int32, (groups, LANES), 1)
    live = lane < jnp.minimum(lists_ref[:, 2, :], cap)
    key = jnp.where(live, lists_ref[:, 1, :] * groups + lists_ref[:, 0, :], -1)
    per_row = LANES // span
    row_lane = lax.broadcasted_iota(jnp.int32, (1, LANES), 1)
    own = jnp.zeros((1, LANES), jnp.float32)
    most = jnp.zeros((1, 1), jnp.float32)
    for chunk in range(groups * groups // LANES):
        times = jnp.zeros((groups, LANES), jnp.float32)
        for slot in range(cap):
            times += jnp.where(key[:, slot : slot + 1] == lane + chunk * LANES, 1.0, 0.0)
        times = jnp.sum(times, axis=0, keepdims=True)
        for place in range(per_row):
            inside = (row_lane >= place * span) & (row_lane < (place + 1) * span)
            count = jnp.sum(jnp.where(inside & (times > 0.0), 1.0, 0.0), axis=1, keepdims=True)
            most = jnp.maximum(most, count)
            turned = pltpu.roll(times, (LANES - place * span) % LANES, 1) if place else times
            own += jnp.where((chip == chunk * per_row + place) & (row_lane < span), turned, 0.0)
    shape = (LANES, LANES)
    down, across = lax.broadcasted_iota(jnp.int32, shape, 0), lax.broadcasted_iota(jnp.int32, shape, 1)
    own_down = jnp.sum(jnp.where(down == across, own, 0.0), axis=1, keepdims=True)
    before = jnp.sum(jnp.where((across < down) & (own > 0.0), 1.0, 0.0), axis=1, keepdims=True)
    here = (before == across.astype(jnp.float32)) & (own_down > 0.0)
    entry = jnp.sum(jnp.where(here, down.astype(jnp.float32), 0.0), axis=0, keepdims=True)
    often = jnp.sum(jnp.where(here, own_down, 0.0), axis=0, keepdims=True)
    row = lax.broadcasted_iota(jnp.int32, (8, LANES), 0)
    return jnp.where(row == 0, entry, jnp.where(row == 1, often, most)).astype(jnp.int32)


def gather_kernel(
    rings, span, orbital_ref, slot_ref, pairs_ref, count_ref, window_ref, list_ref, lists_ref, give, own_list,
    swap_sems, list_send, list_recv, near_send, near_recv, far_send, far_recv,
):
    ring_x, ring_z = rings
    band = lax.axis_index("band")
    groups = lax.axis_size("band")
    core, chip = lax.rem(band, 2), band // 2
    at_x, at_z = chip // ring_z, lax.rem(chip, ring_z)
    packed = window_ref.shape[0] // groups

    barrier = pltpu.get_barrier_semaphore()

    def greet(step, carry):
        pl.semaphore_signal(barrier, inc=1, device_id={"band": lax.rem(band + step, groups)}, device_id_type=MESH)
        return carry

    lax.fori_loop(1, groups, greet, 0)

    part_rows = packed // 3
    quarter = part_rows // 3
    first = slot_ref[0] == 0
    for two in range(3):
        for side in range(2):
            rows = pl.ds(side * (orbital_ref.shape[1] // 2) + two * 4 * quarter, 4 * quarter)
            values = jnp.where(
                first, orbital_ref[0, rows].astype(jnp.float32), orbital_ref[1, rows].astype(jnp.float32)
            )
            last = values[3 * quarter :]
            for third in range(3):
                full = jnp.concatenate(
                    [values[third * quarter : (third + 1) * quarter], last[:, 32 * third : 32 * third + 32]], axis=1
                ).astype(jnp.bfloat16)
                row = two * part_rows + third * quarter

                @pl.when(core == side)
                def _():
                    window_ref[pl.ds(pl.multiple_of(band * packed + row, 16), quarter)] = full

                @pl.when(core != side)
                def _():
                    give[pl.ds(row, quarter)] = full

    own_list[...] = jnp.zeros_like(own_list)
    own_list[0:2, 0 : pairs_ref.shape[1]] = pairs_ref[...]
    own_list[2:3] = jnp.full((1, LANES), count_ref[0], jnp.int32)

    pl.semaphore_wait(barrier, groups - 1)

    def blocks(first_band, count):
        return window_ref.at[pl.ds(pl.multiple_of(first_band * packed, 16), count * packed)]

    def send(src, dst, send_sem, recv_sem, target):
        return pltpu.make_async_remote_copy(
            src_ref=src, dst_ref=dst, send_sem=send_sem, recv_sem=recv_sem,
            device_id={"band": target}, device_id_type=MESH,
        )

    def swap(owner):
        return send(give, blocks(owner, 1), swap_sems.at[0], swap_sems.at[1], band + 1 - 2 * core)

    swap(band).start()

    def send_list(step, owner):
        other = lax.rem(band + step, groups)
        return send(own_list, lists_ref.at[owner], list_send.at[step], list_recv.at[step], other)

    def start_list(step, carry):
        send_list(step, band).start()
        return carry

    def place(x, z):
        return lax.rem(x + ring_x, ring_x) * ring_z + lax.rem(z + ring_z, ring_z)

    level = (0, -1, 1, 2)
    later = packed // 9
    main, rest = (1, 0, 0, packed - later), (0, 1, packed - later, later)
    number = {main: 0, rest: 1}

    def along(plan, ring, step):
        move = [0, 0]
        if ring == 0:
            move[plan[0]] = step
        else:
            move[plan[1]], move[plan[0]] = step, level[ring - 1]
        return place(at_x + move[0], at_z + move[1])

    def neighbour(plan, ring, step):
        move = [0, 0]
        move[plan[min(ring, 1)]] = step
        return 2 * place(at_x + move[0], at_z + move[1]) + core

    def piece(plan, chip_at, half):
        return window_ref.at[pl.ds(pl.multiple_of((2 * chip_at + half) * packed + plan[2], 16), plan[3])]

    def near(plan, ring, way, half):
        block = piece(plan, along(plan, ring, 0), half)
        sems = [sem.at[number[plan], ring, way, half] for sem in (near_send, near_recv)]
        return send(block, block, *sems, neighbour(plan, ring, 1 - 2 * way))

    def far(plan, ring, way):
        block = piece(plan, along(plan, ring, -1 + 2 * way), way)
        sems = [sem.at[number[plan], ring, way] for sem in (far_send, far_recv)]
        return send(block, block, *sems, neighbour(plan, ring, 1 - 2 * way))

    def begin_half(plan, ring, half):
        for way in range(2):
            near(plan, ring, way, half).start()

    def begin(plan, ring):
        for turn in range(2):
            for way in range(2):
                near(plan, ring, way, way if turn == 0 else 1 - way).start()

    def onward(plan, ring, way):
        near(plan, ring, way, way).wait_recv()
        far(plan, ring, way).start()

    swap(band).wait_recv()
    begin(main, 0)
    begin(main, 1)
    begin(rest, 0)
    lax.fori_loop(1, groups, start_list, 0)
    for way in range(2):
        onward(main, 0, way)
        begin_half(main, 2 + way, way)
    for way in range(2):
        onward(rest, 0, way)
        onward(main, 1, way)
    for way in range(2):
        near(main, 0, way, 1 - way).wait_recv()
        begin_half(main, 2 + way, 1 - way)
    for way in range(2):
        far(main, 0, way).wait_recv()
        begin_half(main, 4, way)
    begin(rest, 1)
    for way in range(2):
        near(rest, 0, way, 1 - way).wait_recv()
        begin(rest, 2 + way)
    for turn in range(2):
        for way in range(2):
            onward(main, 2 + way, way if turn == 0 else 1 - way)
    for way in range(2):
        far(rest, 0, way).wait_recv()
    begin(rest, 4)
    for ring in range(1, 4):
        for way in range(2):
            onward(rest, ring, way)

    def end_list(step, carry):
        send_list(step, band).wait_recv()
        send_list(step, band).wait_send()
        return carry

    lax.fori_loop(1, groups, end_list, 0)
    lists_ref[band] = own_list[...]
    list_ref[...] = distinct_tasks(lists_ref, pairs_ref.shape[1], chip)

    for plan in (main, rest):
        for way in range(2):
            onward(plan, 4, way)
    for plan in (main, rest):
        for ring in range(1, 5):
            for way in range(2):
                near(plan, ring, way, 1 - way).wait_recv()
                far(plan, ring, way).wait_recv()
    swap(band).wait_send()
    for plan in (main, rest):
        for ring in range(5):
            for way in range(2):
                near(plan, ring, way, 0).wait_send()
                near(plan, ring, way, 1).wait_send()
                far(plan, ring, way).wait_send()


def gather_window(rings, span, orbitals, window_slot, task_pairs, task_count):
    groups = lax.axis_size("band")
    slab_rows = orbitals.shape[1]
    packed = slab_rows // 2 * span * span // LANES
    smem, vmem = pl.BlockSpec(memory_space=pltpu.SMEM), pl.BlockSpec(memory_space=pltpu.VMEM)
    dma = pltpu.SemaphoreType.DMA
    return pl.pallas_call(
        functools.partial(gather_kernel, rings, span),
        out_shape=(
            jax.ShapeDtypeStruct((groups * packed, LANES), jnp.bfloat16),
            jax.ShapeDtypeStruct((8, LANES), jnp.int32),
        ),
        in_specs=[vmem, smem, vmem, smem],
        out_specs=(vmem, vmem),
        scratch_shapes=[pltpu.VMEM((groups, 8, LANES), jnp.int32)]
        + [pltpu.VMEM((packed, LANES), jnp.bfloat16), pltpu.VMEM((8, LANES), jnp.int32)]
        + [dma((2,)), dma((groups,)), dma((groups,))]
        + [dma((2, 5, 2, 2))] * 2
        + [dma((2, 5, 2))] * 2,
        compiler_params=pltpu.CompilerParams(
            collective_id=9, has_side_effects=True, vmem_limit_bytes=56 * 1024 * 1024
        ),
        name="gather_window",
    )(orbitals.reshape(2, slab_rows * span, span), window_slot, task_pairs[0], task_count)


def on_device(orbitals, exchange_in, window_slot, task_pairs, task_count):
    band_dev, slab_rows, span, _ = orbitals.shape
    grid_parts = lax.axis_size("grid")
    groups = lax.axis_size("band")
    members = 2 * grid_parts
    own_rows = span // members
    window, lists = gather_window((4, 4), span, orbitals, window_slot, task_pairs, task_count)
    window = window.reshape(groups, -1, LANES)
    constants = [jnp.asarray(a) for a in (quarter_kernels(span), undo_emphasis(span), lane_table(span), row_tables(span))]
    most = lists[2, 0]

    def few():
        return run_tasks(3, span, members, jnp.zeros((1,), jnp.int32), lists, window, *constants)

    def many():
        def step(carry):
            start, total = carry
            return start + 16, total + run_tasks(4, span, members, start[None], lists, window, *constants)

        zero = jnp.zeros((2, own_rows * span, LANES), jnp.float32)
        return lax.while_loop(lambda carry: carry[0] < most, step, (jnp.int32(0), zero))[1]

    owned = lax.cond(most <= 12, few, many)
    owned = owned.reshape(slab_rows, span, LANES)[:, :, :span]
    slot_ids = jnp.arange(band_dev, dtype=jnp.int32)[:, None, None, None]
    return exchange_in + jnp.where(slot_ids == window_slot[0], owned, 0.0)


def solution(mesh):
    in_specs = (
        P("band", "grid", None, None),
        P("band", "grid", None, None),
        P("band"),
        P("band", None, None),
        P("band"),
    )
    out_specs = P("band", "grid", None, None)
    return jax.shard_map(
        on_device, mesh=mesh, in_specs=in_specs, out_specs=out_specs, check_vma=False
    )
```

```python
import functools
import math

import jax
import jax.numpy as jnp
import numpy as np
from jax import lax
from jax.experimental import pallas as pl
from jax.experimental.pallas import tpu as pltpu
from jax.sharding import PartitionSpec as P

MESH = pl.DeviceIdType.MESH
LANES = 128
QUAD = 4


def hartley_table(length):
    steps_all = np.arange(length)
    angle = (steps_all[:, None] * steps_all[None, :] % length) * (2.0 * math.pi / length)
    return np.cos(angle) + np.sin(angle)


def split_table(length):
    table = hartley_table(length).astype(np.float32)
    high = table.astype(jnp.bfloat16)
    low = (table - high.astype(np.float32)).astype(jnp.bfloat16)
    return high, low


def lane_table(length):
    high, low = split_table(length)
    out = np.zeros((2 * LANES, 2 * LANES), jnp.bfloat16)
    out[:length, :length] = high
    out[:length, LANES : LANES + length] = low
    out[LANES : LANES + length, :length] = high
    return out


def row_tables(length):
    high, low = split_table(length)
    order = np.arange(length).reshape(-1, 3, 2).transpose(2, 1, 0).reshape(-1)
    out = np.zeros((3, 2 * length, 2 * length), jnp.bfloat16)
    plain = np.arange(length)
    for which, pick in enumerate((np.ix_(plain, plain), np.ix_(plain, order), np.ix_(order, plain))):
        out[which, :length, :length] = high[pick]
        out[which, :length, length:] = high[pick]
        out[which, length:, :length] = low[pick]
    return out


def emphasis(length):
    steps_all = np.arange(length)
    signed = np.where(steps_all <= length // 2, steps_all, steps_all - length).astype(np.float64)
    return ((signed**2)[:, None] + (signed**2)[None, :] + 1.0) ** 0.75


def undo_emphasis(length):
    out = np.zeros((length, LANES), np.float32)
    out[:, :length] = 1.0 / emphasis(length)
    return out


def quarter_kernels(span):
    steps_all = np.arange(span)
    wave = np.where(steps_all <= span // 2, steps_all, steps_all - span) * (2.0 * math.pi / span)
    square = (wave**2)[:, None, None] + (wave**2)[None, :, None] + (wave**2)[None, None, :]
    safe = np.where(square > 0, square, 1.0)
    kernel = np.where(square > 0, 4.0 * math.pi / span**3 / safe, 0.0) * emphasis(span)
    kernel = np.pad(kernel, ((0, 0), (0, 0), (0, LANES - span))).reshape(span, QUAD, span // QUAD, LANES)
    return kernel.transpose(1, 0, 2, 3).reshape(QUAD, -1, LANES).astype(np.float32)


def split(values):
    high = values.astype(jnp.bfloat16)
    return high, (values - high.astype(jnp.float32)).astype(jnp.bfloat16)


def unpack(values):
    rows = values.shape[0] // 3
    parts = [values[third * rows : (third + 1) * rows] for third in range(3)]
    lane = lax.broadcasted_iota(jnp.int32, (rows, LANES), 1)
    turned = [pltpu.roll(parts[third], 32 * (third + 1), 1) for third in range(3)]
    last = jnp.where(lane < 32, turned[0], jnp.where(lane < 64, turned[1], turned[2]))
    return jnp.concatenate([*parts, last], axis=0)


LEVELS = 32766.0
FINE = 2.0**24
STEPS = 256.0
LN2 = math.log(2.0)


def grade(peak):
    return jnp.ceil(jnp.log(jnp.maximum(peak, 1e-30)) * (STEPS / LN2) + 0.01)


def size(graded):
    return jnp.exp(graded * (LN2 / STEPS))


def nearest(values):
    return jnp.round(values).astype(jnp.int32)


def lanes_of(values):
    return lax.broadcasted_iota(jnp.int32, values.shape, 1)


def encode(first, second):
    top = grade(jnp.max(jnp.maximum(jnp.abs(first), jnp.abs(second)), axis=(0, 1), keepdims=True))
    factor = LEVELS / size(top)
    return lax.shift_left(nearest(first * factor), 16) + nearest(second * factor), top.astype(jnp.int32)


def encode_apart(first, second):
    lane = lax.broadcasted_iota(jnp.int32, (1, LANES), 1)
    peaks = jnp.max(jnp.maximum(jnp.abs(first), jnp.abs(second)), axis=0, keepdims=True)
    top = grade(jnp.max(jnp.where(lane > 0, peaks, 0.0), axis=1, keepdims=True))
    high = grade(jnp.max(jnp.where(lane > 0, 0.0, peaks), axis=1, keepdims=True))
    factor = jnp.where(lane > 0, LEVELS / size(top), FINE / size(high))
    first, second = nearest(first * factor), nearest(second * factor)
    word = jnp.where(lanes_of(first) > 0, lax.shift_left(first, 16) + second, first)
    return word, second, top.astype(jnp.int32), high.astype(jnp.int32)


def halves(word):
    second = lax.shift_right_arithmetic(lax.shift_left(word, 16), 16)
    return lax.shift_right_arithmetic(word - second, 16), second


def decode(word, scale):
    return [half.astype(jnp.float32) * scale for half in halves(word)]


def decode_apart(word, second_apart, scale):
    lane = lanes_of(word)
    first, second = halves(word)
    first, second = jnp.where(lane > 0, first, word), jnp.where(lane > 0, second, second_apart)
    return [first.astype(jnp.float32) * scale, second.astype(jnp.float32) * scale]


def beside(full, third, turn):
    return jnp.where(lanes_of(full) < 96, full, pltpu.roll(third, turn, 1))


def tail_lanes(pieces):
    lane = lanes_of(pieces[0])
    first, second = pltpu.roll(pieces[0], 64, 1), pltpu.roll(pieces[1], 96, 1)
    return jnp.where(lane < 32, first, jnp.where(lane < 64, second, pieces[2]))


def third_of(full, second_full, tail, group):
    lane = lanes_of(full)
    last = pltpu.roll(tail, 64 - 32 * group, 1) if group < 2 else tail
    return jnp.where(lane < 32, pltpu.roll(full, 32, 1), jnp.where(lane < 64, pltpu.roll(second_full, 64, 1), last))


def put(values, lane_at, column):
    return jnp.where(lanes_of(values) == lane_at, column, values)


def along_lanes(values, table):
    both = jnp.dot(jnp.concatenate(split(values), axis=1), table, preferred_element_type=jnp.float32)
    return both[:, :LANES] + both[:, LANES:]


def along_rows(values, table):
    both = jnp.dot(table, jnp.concatenate(split(values), axis=0), preferred_element_type=jnp.float32)
    span = values.shape[0]
    return both[:span] + both[span:]


def task_kernel(
    quads, span, start_ref, list_ref, window_ref, kernels_ref, undo_ref, lane_ref, row_ref, out_ref,
    kernel_ref, send_out, recv_out, send_back, recv_back, total, partner_part,
    out_send_sem, out_recv_sem, back_send_sem, back_recv_sem, part_sems, kernel_sem,
):
    band = lax.axis_index("band")
    core = lax.rem(band, 2)
    pair = band - core
    members = 2 * lax.axis_size("grid")
    me = 2 * lax.axis_index("grid") + core
    own_rows = span // members
    rows = span // QUAD
    block = 2 * rows + rows // 3
    eighth = rows // 3
    my_slot = me // QUAD

    def place(member):
        return {"band": pair + lax.rem(member, 2), "grid": member // 2}

    kernel_copy = pltpu.make_async_copy(kernels_ref.at[lax.rem(me, QUAD)], kernel_ref, kernel_sem.at[0])
    kernel_copy.start()
    barrier = pltpu.get_barrier_semaphore()

    def greet(step, carry):
        pl.semaphore_signal(barrier, inc=1, device_id=place(lax.rem(me + step, members)), device_id_type=MESH)
        return carry

    lax.fori_loop(1, members, greet, 0)

    def at(ref, quad, member):
        return ref.at[quad, pl.ds(pl.multiple_of(member * block, 8), block)]

    def remote(quad, member, origin, src, dst, send_sem, recv_sem):
        return pltpu.make_async_remote_copy(
            src_ref=at(src, quad, member), dst_ref=at(dst, quad, origin),
            send_sem=send_sem.at[quad, member], recv_sem=recv_sem.at[quad, origin],
            device_id=place(member), device_id_type=MESH,
        )

    def local(quad, src, dst, recv_sem):
        return pltpu.make_async_copy(at(src, quad, me), at(dst, quad, me), recv_sem.at[quad, me])

    def start_one(quad, member, src, dst, send_sem, recv_sem):
        @pl.when(member != me)
        def _():
            remote(quad, member, me, src, dst, send_sem, recv_sem).start()

        @pl.when(member == me)
        def _():
            local(quad, src, dst, recv_sem).start()

    def start_all(quad, *way):
        def step_one(step, carry):
            start_one(quad, lax.rem(me + step, members), *way)
            return carry

        lax.fori_loop(1, members + 1, step_one, 0)

    def wait_one(quad, member, src, dst, send_sem, recv_sem):
        @pl.when(member != me)
        def _():
            remote(quad, member, member, src, dst, send_sem, recv_sem).wait_recv()

        @pl.when(member == me)
        def _():
            local(quad, src, dst, recv_sem).wait()

    def wait_recv(quad, *way):
        def step_one(step, carry):
            wait_one(quad, lax.rem(me + step, members), *way)
            return carry

        lax.fori_loop(1, members + 1, step_one, 0)

    def wait_send(quad, src, dst, send_sem, recv_sem):
        def step_one(step, carry):
            other = lax.rem(me + step, members)
            remote(quad, other, me, src, dst, send_sem, recv_sem).wait_send()
            return carry

        lax.fori_loop(1, members, step_one, 0)

    outward = (send_out, recv_out, out_send_sem, out_recv_sem)
    backward = (send_back, recv_back, back_send_sem, back_recv_sem)

    packed = window_ref.shape[1] // (own_rows // 2)

    def window_part(position, two):
        return window_ref[position, pl.ds(two * packed, packed)].astype(jnp.float32)

    def task(quad, slot):
        index = start_ref[0] + quad * QUAD + slot
        entry = list_ref[0, index]
        groups = lax.axis_size("band")
        return lax.rem(entry, groups), entry // groups, list_ref[1, index].astype(jnp.float32)

    def inner(quad):
        def one(step, carry):
            slot = lax.rem(my_slot + 1 + step, QUAD)
            source, side, _ = task(quad, slot)
            target = pair + side
            parts = range(own_rows // 2)
            mixed = [along_lanes(unpack(window_part(source, two) * window_part(target, two)), lane_ref[...]) for two in parts]
            mixed = [along_rows(jnp.concatenate([value[:span], value[span:]], axis=1), row_ref[0]) for value in mixed]
            coded = [encode_apart(value[:, :LANES], value[:, LANES:]) for value in mixed]
            words, seconds, tops, highs = zip(*coded)
            for quarter in range(QUAD):
                start = (slot * QUAD + quarter) * block
                here = slice(quarter * rows, (quarter + 1) * rows)
                third = words[2][here]
                groups = [slice(quarter * rows + g * eighth, quarter * rows + (g + 1) * eighth) for g in range(3)]
                tail = tail_lanes([words[2][group] for group in groups])
                for two in parts:
                    for g, group in enumerate(groups):
                        at_lane = 96 + 3 * two + g
                        tail = put(tail, at_lane, pltpu.roll(seconds[two][group], at_lane, 1))
                    tail = put(put(tail, 105 + 2 * two, tops[two]), 106 + 2 * two, highs[two])
                send_out[quad, pl.ds(pl.multiple_of(start, 8), rows)] = beside(words[0][here], third, 96)
                send_out[quad, pl.ds(pl.multiple_of(start + rows, 8), rows)] = beside(words[1][here], third, 64)
                send_out[quad, pl.ds(pl.multiple_of(start + 2 * rows, 8), eighth)] = tail
            for quarter in range(QUAD):
                start_one(quad, slot * QUAD + quarter, *outward)
            return carry

        lax.fori_loop(0, QUAD, one, 0)

    def outer(quad):
        wait_recv(quad, *outward)

        def across(first):
            return pl.ds(first, members, stride=block)

        tail = recv_out[quad, across(2 * rows)]
        scales = []
        for two in range(3):
            rest = size(tail[:, 105 + 2 * two : 106 + 2 * two].astype(jnp.float32)) * (1.0 / LEVELS)
            mean = size(tail[:, 106 + 2 * two : 107 + 2 * two].astype(jnp.float32)) * (1.0 / FINE)
            scales.append(jnp.where(lanes_of(tail) > 0, rest, mean))
        scale = jnp.concatenate(scales, axis=0)

        def some(step, carry):
            tails = [recv_out[quad, across(2 * rows + 2 * step + half)] for half in range(2)]
            values = []
            for g in range(3):
                both = []
                for half in range(2):
                    row = g * eighth + 2 * step + half
                    first, second = recv_out[quad, across(row)], recv_out[quad, across(rows + row)]
                    word = jnp.concatenate([first, second, third_of(first, second, tails[half], g)], axis=0)
                    apart = jnp.concatenate([pltpu.roll(tails[half], 32 - 3 * two - g, 1) for two in range(3)], axis=0)
                    both.append(jnp.concatenate(decode_apart(word, apart, scale), axis=0))
                values.append(jnp.concatenate(both, axis=1))
            mixed = [along_rows(value, row_ref[1]) for value in values]
            factors = [
                jnp.concatenate(
                    [kernel_ref[pl.ds(g * eighth + 2 * step + half, span, stride=rows)] for half in range(2)], axis=1
                )
                for g in range(3)
            ]
            restored = [along_rows(value * factor, row_ref[2]) for value, factor in zip(mixed, factors)]
            for half in range(2):
                side = slice(half * LANES, (half + 1) * LANES)
                words, tops = zip(*[encode(value[: span // 2, side], value[span // 2 :, side]) for value in restored])
                thirds = [word[2 * members :] for word in words]
                tail = tail_lanes(thirds)
                for g in range(3):
                    row = g * eighth + 2 * step + half
                    tail = put(tail, 96 + g, tops[g])
                    send_back[quad, across(row)] = beside(words[g][:members], thirds[g], 96)
                    send_back[quad, across(rows + row)] = beside(words[g][members : 2 * members], thirds[g], 64)
                send_back[quad, across(2 * rows + 2 * step + half)] = tail
            return carry

        lax.fori_loop(0, eighth // 2, some, 0)
        start_all(quad, *backward)

    def finish(quad):
        def one(step, carry):
            slot = lax.rem(my_slot + step, QUAD)
            source, wanted, often = task(quad, slot)
            weights = [jnp.where(wanted == side, often, 0.0) for side in range(2)]
            words, scales = [[], [], []], []
            for quarter in range(QUAD):
                wait_one(quad, slot * QUAD + quarter, *backward)
            for quarter in range(QUAD):
                start = (slot * QUAD + quarter) * block
                first, second = [
                    recv_back[quad, pl.ds(pl.multiple_of(start + two * rows, 8), rows)] for two in range(2)
                ]
                tail = recv_back[quad, pl.ds(pl.multiple_of(start + 2 * rows, 8), eighth)]
                words[0].append(first)
                words[1].append(second)
                for g in range(3):
                    group = slice(g * eighth, (g + 1) * eighth)
                    words[2].append(third_of(first[group], second[group], tail, g))
                    scales.append(tail[:, 96 + g : 97 + g])
            scale = size(jnp.concatenate(scales, axis=0).astype(jnp.float32)) * (1.0 / LEVELS) * undo_ref[...]
            parts = range(own_rows // 2)
            mixed = [jnp.concatenate(decode(jnp.concatenate(words[two], axis=0), scale), axis=1) for two in parts]
            mixed = [along_rows(value, row_ref[0]) for value in mixed]
            potentials = [
                along_lanes(jnp.concatenate([value[:, :LANES], value[:, LANES:]], axis=0), lane_ref[...]) for value in mixed
            ]
            for two in parts:
                part = pl.ds(2 * two * span, 2 * span)
                action = potentials[two] * unpack(window_part(source, two))
                for side in range(2):
                    total[side, part] += action * weights[side]
            return carry

        lax.fori_loop(0, QUAD, one, 0)

    total[...] = jnp.zeros_like(total)
    pl.semaphore_wait(barrier, members - 1)
    for quad in range(quads):
        inner(quad)
    kernel_copy.wait()
    for quad in range(quads):
        outer(quad)
    for quad in range(quads):
        finish(quad)

    swap = pltpu.make_async_remote_copy(
        src_ref=total.at[1 - core], dst_ref=partner_part, send_sem=part_sems.at[0], recv_sem=part_sems.at[1],
        device_id={"band": pair + 1 - core, "grid": lax.axis_index("grid")}, device_id_type=MESH,
    )
    swap.start()
    out_ref[core] = total[core]
    swap.wait_recv()
    out_ref[1 - core] = partner_part[...]
    swap.wait_send()
    for quad in range(quads):
        wait_send(quad, *outward)
        wait_send(quad, *backward)


def run_tasks(quads, span, members, *operands):
    own_rows = span // members
    whole = (quads, members * (span // QUAD) * 7 // 3, LANES)
    smem, vmem = pl.BlockSpec(memory_space=pltpu.SMEM), pl.BlockSpec(memory_space=pltpu.VMEM)
    sems = pltpu.SemaphoreType.DMA((quads, members))
    return pl.pallas_call(
        functools.partial(task_kernel, quads, span),
        out_shape=jax.ShapeDtypeStruct((2, own_rows * span, LANES), jnp.float32),
        in_specs=[smem] * 2 + [vmem] + [pl.BlockSpec(memory_space=pl.ANY)] + [vmem] * 3,
        out_specs=vmem,
        scratch_shapes=[pltpu.VMEM((span * span // QUAD, LANES), jnp.float32)]
        + [pltpu.VMEM(whole, jnp.int32)] * 4
        + [pltpu.VMEM((2, own_rows * span, LANES), jnp.float32), pltpu.VMEM((own_rows * span, LANES), jnp.float32)]
        + [sems] * 4
        + [pltpu.SemaphoreType.DMA((2,)), pltpu.SemaphoreType.DMA((1,))],
        compiler_params=pltpu.CompilerParams(
            collective_id=quads, has_side_effects=True, vmem_limit_bytes=56 * 1024 * 1024
        ),
        name="exchange_tasks",
    )(*operands)


def distinct_tasks(lists_ref, cap, chip):
    groups = lists_ref.shape[0]
    span = 2 * groups
    lane = lax.broadcasted_iota(jnp.int32, (groups, LANES), 1)
    live = lane < jnp.minimum(lists_ref[:, 2, :], cap)
    key = jnp.where(live, lists_ref[:, 1, :] * groups + lists_ref[:, 0, :], -1)
    per_row = LANES // span
    row_lane = lax.broadcasted_iota(jnp.int32, (1, LANES), 1)
    own = jnp.zeros((1, LANES), jnp.float32)
    most = jnp.zeros((1, 1), jnp.float32)
    for chunk in range(groups * groups // LANES):
        times = jnp.zeros((groups, LANES), jnp.float32)
        for slot in range(cap):
            times += jnp.where(key[:, slot : slot + 1] == lane + chunk * LANES, 1.0, 0.0)
        times = jnp.sum(times, axis=0, keepdims=True)
        for place in range(per_row):
            inside = (row_lane >= place * span) & (row_lane < (place + 1) * span)
            count = jnp.sum(jnp.where(inside & (times > 0.0), 1.0, 0.0), axis=1, keepdims=True)
            most = jnp.maximum(most, count)
            turned = pltpu.roll(times, (LANES - place * span) % LANES, 1) if place else times
            own += jnp.where((chip == chunk * per_row + place) & (row_lane < span), turned, 0.0)
    shape = (LANES, LANES)
    down, across = lax.broadcasted_iota(jnp.int32, shape, 0), lax.broadcasted_iota(jnp.int32, shape, 1)
    own_down = jnp.sum(jnp.where(down == across, own, 0.0), axis=1, keepdims=True)
    before = jnp.sum(jnp.where((across < down) & (own > 0.0), 1.0, 0.0), axis=1, keepdims=True)
    here = (before == across.astype(jnp.float32)) & (own_down > 0.0)
    entry = jnp.sum(jnp.where(here, down.astype(jnp.float32), 0.0), axis=0, keepdims=True)
    often = jnp.sum(jnp.where(here, own_down, 0.0), axis=0, keepdims=True)
    row = lax.broadcasted_iota(jnp.int32, (8, LANES), 0)
    return jnp.where(row == 0, entry, often).astype(jnp.int32), most


def gather_kernel(
    rings, span, orbital_ref, slot_ref, pairs_ref, count_ref, window_ref, list_ref, most_ref, lists_ref, give, own_list,
    swap_sems, list_send, list_recv, near_send, near_recv, far_send, far_recv,
):
    ring_x, ring_z = rings
    band = lax.axis_index("band")
    groups = lax.axis_size("band")
    core, chip = lax.rem(band, 2), band // 2
    at_x, at_z = chip // ring_z, lax.rem(chip, ring_z)
    packed = window_ref.shape[0] // groups

    barrier = pltpu.get_barrier_semaphore()

    def greet(step, carry):
        pl.semaphore_signal(barrier, inc=1, device_id={"band": lax.rem(band + step, groups)}, device_id_type=MESH)
        return carry

    lax.fori_loop(1, groups, greet, 0)

    part_rows = packed // 3
    quarter = part_rows // 3
    first = slot_ref[0] == 0
    for two in range(3):
        for side in range(2):
            rows = pl.ds(side * (orbital_ref.shape[1] // 2) + two * 4 * quarter, 4 * quarter)
            values = jnp.where(
                first, orbital_ref[0, rows].astype(jnp.float32), orbital_ref[1, rows].astype(jnp.float32)
            )
            last = values[3 * quarter :]
            for third in range(3):
                full = jnp.concatenate(
                    [values[third * quarter : (third + 1) * quarter], last[:, 32 * third : 32 * third + 32]], axis=1
                ).astype(jnp.bfloat16)
                row = two * part_rows + third * quarter

                @pl.when(core == side)
                def _():
                    window_ref[pl.ds(pl.multiple_of(band * packed + row, 16), quarter)] = full

                @pl.when(core != side)
                def _():
                    give[pl.ds(row, quarter)] = full

    own_list[...] = jnp.zeros_like(own_list)
    own_list[0:2, 0 : pairs_ref.shape[1]] = pairs_ref[...]
    own_list[2:3] = jnp.full((1, LANES), count_ref[0], jnp.int32)

    pl.semaphore_wait(barrier, groups - 1)

    def blocks(first_band, count):
        return window_ref.at[pl.ds(pl.multiple_of(first_band * packed, 16), count * packed)]

    def send(src, dst, send_sem, recv_sem, target):
        return pltpu.make_async_remote_copy(
            src_ref=src, dst_ref=dst, send_sem=send_sem, recv_sem=recv_sem,
            device_id={"band": target}, device_id_type=MESH,
        )

    def swap(owner):
        return send(give, blocks(owner, 1), swap_sems.at[0], swap_sems.at[1], band + 1 - 2 * core)

    swap(band).start()

    def send_list(step, owner):
        other = lax.rem(band + step, groups)
        return send(own_list, lists_ref.at[owner], list_send.at[step], list_recv.at[step], other)

    def start_list(step, carry):
        send_list(step, band).start()
        return carry

    def place(x, z):
        return lax.rem(x + ring_x, ring_x) * ring_z + lax.rem(z + ring_z, ring_z)

    level = (0, -1, 1, 2)
    later = packed // 9
    main, rest = (1, 0, 0, packed - later), (0, 1, packed - later, later)
    number = {main: 0, rest: 1}

    def along(plan, ring, step):
        move = [0, 0]
        if ring == 0:
            move[plan[0]] = step
        else:
            move[plan[1]], move[plan[0]] = step, level[ring - 1]
        return place(at_x + move[0], at_z + move[1])

    def neighbour(plan, ring, step):
        move = [0, 0]
        move[plan[min(ring, 1)]] = step
        return 2 * place(at_x + move[0], at_z + move[1]) + core

    def piece(plan, chip_at, half):
        return window_ref.at[pl.ds(pl.multiple_of((2 * chip_at + half) * packed + plan[2], 16), plan[3])]

    def near(plan, ring, way, half):
        block = piece(plan, along(plan, ring, 0), half)
        sems = [sem.at[number[plan], ring, way, half] for sem in (near_send, near_recv)]
        return send(block, block, *sems, neighbour(plan, ring, 1 - 2 * way))

    def far(plan, ring, way):
        block = piece(plan, along(plan, ring, -1 + 2 * way), way)
        sems = [sem.at[number[plan], ring, way] for sem in (far_send, far_recv)]
        return send(block, block, *sems, neighbour(plan, ring, 1 - 2 * way))

    def begin_half(plan, ring, half):
        for way in range(2):
            near(plan, ring, way, half).start()

    def begin(plan, ring):
        for turn in range(2):
            for way in range(2):
                near(plan, ring, way, way if turn == 0 else 1 - way).start()

    def onward(plan, ring, way):
        near(plan, ring, way, way).wait_recv()
        far(plan, ring, way).start()

    for ring in range(2):
        begin_half(main, ring, core)
    swap(band).wait_recv()
    for ring in range(2):
        begin_half(main, ring, 1 - core)
    begin(rest, 0)
    lax.fori_loop(1, groups, start_list, 0)
    for way in range(2):
        onward(main, 0, way)
        begin_half(main, 2 + way, way)
    for way in range(2):
        onward(rest, 0, way)
        onward(main, 1, way)
    for way in range(2):
        near(main, 0, way, 1 - way).wait_recv()
        begin_half(main, 2 + way, 1 - way)
    for way in range(2):
        far(main, 0, way).wait_recv()
        begin_half(main, 4, way)
    begin(rest, 1)
    for way in range(2):
        near(rest, 0, way, 1 - way).wait_recv()
        begin(rest, 2 + way)
    for turn in range(2):
        for way in range(2):
            onward(main, 2 + way, way if turn == 0 else 1 - way)
    for way in range(2):
        far(rest, 0, way).wait_recv()
    begin(rest, 4)
    for ring in range(1, 4):
        for way in range(2):
            onward(rest, ring, way)

    def end_list(step, carry):
        send_list(step, band).wait_recv()
        send_list(step, band).wait_send()
        return carry

    lax.fori_loop(1, groups, end_list, 0)
    lists_ref[band] = own_list[...]
    list_ref[...], most = distinct_tasks(lists_ref, pairs_ref.shape[1], chip)
    most_ref[0] = jnp.max(most).astype(jnp.int32)

    for plan in (main, rest):
        for way in range(2):
            onward(plan, 4, way)
    for plan in (main, rest):
        for ring in range(1, 5):
            for way in range(2):
                near(plan, ring, way, 1 - way).wait_recv()
                far(plan, ring, way).wait_recv()
    swap(band).wait_send()
    for plan in (main, rest):
        for ring in range(5):
            for way in range(2):
                near(plan, ring, way, 0).wait_send()
                near(plan, ring, way, 1).wait_send()
                far(plan, ring, way).wait_send()


def gather_window(rings, span, orbitals, window_slot, task_pairs, task_count):
    groups = lax.axis_size("band")
    slab_rows = orbitals.shape[1]
    packed = slab_rows // 2 * span * span // LANES
    smem, vmem = pl.BlockSpec(memory_space=pltpu.SMEM), pl.BlockSpec(memory_space=pltpu.VMEM)
    dma = pltpu.SemaphoreType.DMA
    return pl.pallas_call(
        functools.partial(gather_kernel, rings, span),
        out_shape=(
            jax.ShapeDtypeStruct((groups * packed, LANES), jnp.bfloat16),
            jax.ShapeDtypeStruct((8, LANES), jnp.int32),
            jax.ShapeDtypeStruct((1,), jnp.int32),
        ),
        in_specs=[vmem, smem, vmem, smem],
        out_specs=(vmem, vmem, smem),
        scratch_shapes=[pltpu.VMEM((groups, 8, LANES), jnp.int32)]
        + [pltpu.VMEM((packed, LANES), jnp.bfloat16), pltpu.VMEM((8, LANES), jnp.int32)]
        + [dma((2,)), dma((groups,)), dma((groups,))]
        + [dma((2, 5, 2, 2))] * 2
        + [dma((2, 5, 2))] * 2,
        compiler_params=pltpu.CompilerParams(
            collective_id=9, has_side_effects=True, vmem_limit_bytes=56 * 1024 * 1024
        ),
        name="gather_window",
    )(orbitals.reshape(2, slab_rows * span, span), window_slot, task_pairs[0], task_count)


def on_device(orbitals, exchange_in, window_slot, task_pairs, task_count):
    band_dev, slab_rows, span, _ = orbitals.shape
    grid_parts = lax.axis_size("grid")
    groups = lax.axis_size("band")
    members = 2 * grid_parts
    own_rows = span // members
    window, lists, most = gather_window((4, 4), span, orbitals, window_slot, task_pairs, task_count)
    window = window.reshape(groups, -1, LANES)
    constants = [jnp.asarray(a) for a in (quarter_kernels(span), undo_emphasis(span), lane_table(span), row_tables(span))]
    most = most[0]

    def few():
        return run_tasks(3, span, members, jnp.zeros((1,), jnp.int32), lists, window, *constants)

    def many():
        def step(carry):
            start, total = carry
            return start + 16, total + run_tasks(4, span, members, start[None], lists, window, *constants)

        zero = jnp.zeros((2, own_rows * span, LANES), jnp.float32)
        return lax.while_loop(lambda carry: carry[0] < most, step, (jnp.int32(0), zero))[1]

    owned = lax.cond(most <= 12, few, many)
    owned = owned.reshape(slab_rows, span, LANES)[:, :, :span]
    slot_ids = jnp.arange(band_dev, dtype=jnp.int32)[:, None, None, None]
    return exchange_in + jnp.where(slot_ids == window_slot[0], owned, 0.0)


def solution(mesh):
    in_specs = (
        P("band", "grid", None, None),
        P("band", "grid", None, None),
        P("band"),
        P("band", None, None),
        P("band"),
    )
    out_specs = P("band", "grid", None, None)
    return jax.shard_map(
        on_device, mesh=mesh, in_specs=in_specs, out_specs=out_specs, check_vma=False
    )
```

```python
import functools
import math

import jax
import jax.numpy as jnp
import numpy as np
from jax import lax
from jax.experimental import pallas as pl
from jax.experimental.pallas import tpu as pltpu
from jax.sharding import PartitionSpec as P

MESH = pl.DeviceIdType.MESH
LANES = 128
QUAD = 4


def hartley_table(length):
    steps_all = np.arange(length)
    angle = (steps_all[:, None] * steps_all[None, :] % length) * (2.0 * math.pi / length)
    return np.cos(angle) + np.sin(angle)


def split_table(length):
    table = hartley_table(length).astype(np.float32)
    high = table.astype(jnp.bfloat16)
    low = (table - high.astype(np.float32)).astype(jnp.bfloat16)
    return high, low


def lane_table(length):
    high, low = split_table(length)
    out = np.zeros((2 * LANES, 2 * LANES), jnp.bfloat16)
    out[:length, :length] = high
    out[:length, LANES : LANES + length] = low
    out[LANES : LANES + length, :length] = high
    return out


def row_tables(length):
    high, low = split_table(length)
    order = np.arange(length).reshape(-1, 3, 2).transpose(2, 1, 0).reshape(-1)
    out = np.zeros((3, 2 * length, 2 * length), jnp.bfloat16)
    plain = np.arange(length)
    for which, pick in enumerate((np.ix_(plain, plain), np.ix_(plain, order), np.ix_(order, plain))):
        out[which, :length, :length] = high[pick]
        out[which, :length, length:] = high[pick]
        out[which, length:, :length] = low[pick]
    return out


def emphasis(length):
    steps_all = np.arange(length)
    signed = np.where(steps_all <= length // 2, steps_all, steps_all - length).astype(np.float64)
    return ((signed**2)[:, None] + (signed**2)[None, :] + 1.0) ** 0.75


def undo_emphasis(length):
    out = np.zeros((length, LANES), np.float32)
    out[:, :length] = 1.0 / emphasis(length)
    return out


def quarter_kernels(span):
    steps_all = np.arange(span)
    wave = np.where(steps_all <= span // 2, steps_all, steps_all - span) * (2.0 * math.pi / span)
    square = (wave**2)[:, None, None] + (wave**2)[None, :, None] + (wave**2)[None, None, :]
    safe = np.where(square > 0, square, 1.0)
    kernel = np.where(square > 0, 4.0 * math.pi / span**3 / safe, 0.0) * emphasis(span)
    kernel = np.pad(kernel, ((0, 0), (0, 0), (0, LANES - span))).reshape(span, QUAD, span // QUAD, LANES)
    return kernel.transpose(1, 0, 2, 3).reshape(QUAD, -1, LANES).astype(np.float32)


def split(values):
    high = values.astype(jnp.bfloat16)
    return high, (values - high.astype(jnp.float32)).astype(jnp.bfloat16)


def unpack(values):
    rows = values.shape[0] // 3
    parts = [values[third * rows : (third + 1) * rows] for third in range(3)]
    lane = lax.broadcasted_iota(jnp.int32, (rows, LANES), 1)
    turned = [pltpu.roll(parts[third], 32 * (third + 1), 1) for third in range(3)]
    last = jnp.where(lane < 32, turned[0], jnp.where(lane < 64, turned[1], turned[2]))
    return jnp.concatenate([*parts, last], axis=0)


LEVELS = 32766.0
FINE = 2.0**24
STEPS = 256.0
LN2 = math.log(2.0)


def grade(peak):
    return jnp.ceil(jnp.log(jnp.maximum(peak, 1e-30)) * (STEPS / LN2) + 0.01)


def size(graded):
    return jnp.exp(graded * (LN2 / STEPS))


def nearest(values):
    return jnp.round(values).astype(jnp.int32)


def lanes_of(values):
    return lax.broadcasted_iota(jnp.int32, values.shape, 1)


def encode(first, second):
    top = grade(jnp.max(jnp.maximum(jnp.abs(first), jnp.abs(second)), axis=(0, 1), keepdims=True))
    factor = LEVELS / size(top)
    return lax.shift_left(nearest(first * factor), 16) + nearest(second * factor), top.astype(jnp.int32)


def encode_apart(first, second):
    lane = lax.broadcasted_iota(jnp.int32, (1, LANES), 1)
    peaks = jnp.max(jnp.maximum(jnp.abs(first), jnp.abs(second)), axis=0, keepdims=True)
    top = grade(jnp.max(jnp.where(lane > 0, peaks, 0.0), axis=1, keepdims=True))
    high = grade(jnp.max(jnp.where(lane > 0, 0.0, peaks), axis=1, keepdims=True))
    factor = jnp.where(lane > 0, LEVELS / size(top), FINE / size(high))
    first, second = nearest(first * factor), nearest(second * factor)
    word = jnp.where(lanes_of(first) > 0, lax.shift_left(first, 16) + second, first)
    return word, second, top.astype(jnp.int32), high.astype(jnp.int32)


def halves(word):
    second = lax.shift_right_arithmetic(lax.shift_left(word, 16), 16)
    return lax.shift_right_arithmetic(word - second, 16), second


def decode(word, scale):
    return [half.astype(jnp.float32) * scale for half in halves(word)]


def decode_apart(word, second_apart, scale):
    lane = lanes_of(word)
    first, second = halves(word)
    first, second = jnp.where(lane > 0, first, word), jnp.where(lane > 0, second, second_apart)
    return [first.astype(jnp.float32) * scale, second.astype(jnp.float32) * scale]


def beside(full, third, turn):
    return jnp.where(lanes_of(full) < 96, full, pltpu.roll(third, turn, 1))


def tail_lanes(pieces):
    lane = lanes_of(pieces[0])
    first, second = pltpu.roll(pieces[0], 64, 1), pltpu.roll(pieces[1], 96, 1)
    return jnp.where(lane < 32, first, jnp.where(lane < 64, second, pieces[2]))


def third_of(full, second_full, tail, group):
    lane = lanes_of(full)
    last = pltpu.roll(tail, 64 - 32 * group, 1) if group < 2 else tail
    return jnp.where(lane < 32, pltpu.roll(full, 32, 1), jnp.where(lane < 64, pltpu.roll(second_full, 64, 1), last))


def put(values, lane_at, column):
    return jnp.where(lanes_of(values) == lane_at, column, values)


def along_lanes(values, table):
    both = jnp.dot(jnp.concatenate(split(values), axis=1), table, preferred_element_type=jnp.float32)
    return both[:, :LANES] + both[:, LANES:]


def along_rows(values, table):
    both = jnp.dot(table, jnp.concatenate(split(values), axis=0), preferred_element_type=jnp.float32)
    span = values.shape[0]
    return both[:span] + both[span:]


def task_kernel(
    quads, span, start_ref, list_ref, window_ref, kernels_ref, undo_ref, lane_ref, row_ref, out_ref,
    kernel_ref, send_out, recv_out, send_back, recv_back, total, partner_part,
    out_send_sem, out_recv_sem, back_send_sem, back_recv_sem, part_sems, kernel_sem,
):
    band = lax.axis_index("band")
    core = lax.rem(band, 2)
    pair = band - core
    members = 2 * lax.axis_size("grid")
    me = 2 * lax.axis_index("grid") + core
    own_rows = span // members
    rows = span // QUAD
    block = 2 * rows + rows // 3
    eighth = rows // 3
    my_slot = me // QUAD

    def place(member):
        return {"band": pair + lax.rem(member, 2), "grid": member // 2}

    kernel_copy = pltpu.make_async_copy(kernels_ref.at[lax.rem(me, QUAD)], kernel_ref, kernel_sem.at[0])
    kernel_copy.start()
    barrier = pltpu.get_barrier_semaphore()

    def greet(step, carry):
        pl.semaphore_signal(barrier, inc=1, device_id=place(lax.rem(me + step, members)), device_id_type=MESH)
        return carry

    lax.fori_loop(1, members, greet, 0)

    def at(ref, quad, member):
        return ref.at[quad, pl.ds(pl.multiple_of(member * block, 8), block)]

    def remote(quad, member, origin, src, dst, send_sem, recv_sem):
        return pltpu.make_async_remote_copy(
            src_ref=at(src, quad, member), dst_ref=at(dst, quad, origin),
            send_sem=send_sem.at[quad, member], recv_sem=recv_sem.at[quad, origin],
            device_id=place(member), device_id_type=MESH,
        )

    def local(quad, src, dst, recv_sem):
        return pltpu.make_async_copy(at(src, quad, me), at(dst, quad, me), recv_sem.at[quad, me])

    def start_one(quad, member, src, dst, send_sem, recv_sem):
        @pl.when(member != me)
        def _():
            remote(quad, member, me, src, dst, send_sem, recv_sem).start()

        @pl.when(member == me)
        def _():
            local(quad, src, dst, recv_sem).start()

    def start_all(quad, *way):
        def step_one(step, carry):
            start_one(quad, lax.rem(me + step, members), *way)
            return carry

        lax.fori_loop(1, members + 1, step_one, 0)

    def wait_one(quad, member, src, dst, send_sem, recv_sem):
        @pl.when(member != me)
        def _():
            remote(quad, member, member, src, dst, send_sem, recv_sem).wait_recv()

        @pl.when(member == me)
        def _():
            local(quad, src, dst, recv_sem).wait()

    def wait_recv(quad, *way):
        def step_one(step, carry):
            wait_one(quad, lax.rem(me + step, members), *way)
            return carry

        lax.fori_loop(1, members + 1, step_one, 0)

    def wait_send(quad, src, dst, send_sem, recv_sem):
        def step_one(step, carry):
            other = lax.rem(me + step, members)
            remote(quad, other, me, src, dst, send_sem, recv_sem).wait_send()
            return carry

        lax.fori_loop(1, members, step_one, 0)

    outward = (send_out, recv_out, out_send_sem, out_recv_sem)
    backward = (send_back, recv_back, back_send_sem, back_recv_sem)

    packed = window_ref.shape[1] // (own_rows // 2)

    def window_part(position, two):
        return window_ref[position, pl.ds(two * packed, packed)].astype(jnp.float32)

    def task(quad, slot):
        index = start_ref[0] + quad * QUAD + slot
        entry = list_ref[0, index]
        groups = lax.axis_size("band")
        return lax.rem(entry, groups), entry // groups, list_ref[1, index].astype(jnp.float32)

    def inner(quad):
        def one(step, carry):
            slot = lax.rem(my_slot + 1 + step, QUAD)
            source, side, _ = task(quad, slot)
            target = pair + side
            parts = range(own_rows // 2)
            mixed = [along_lanes(unpack(window_part(source, two) * window_part(target, two)), lane_ref[...]) for two in parts]
            mixed = [along_rows(jnp.concatenate([value[:span], value[span:]], axis=1), row_ref[0]) for value in mixed]
            coded = [encode_apart(value[:, :LANES], value[:, LANES:]) for value in mixed]
            words, seconds, tops, highs = zip(*coded)
            for quarter in range(QUAD):
                start = (slot * QUAD + quarter) * block
                here = slice(quarter * rows, (quarter + 1) * rows)
                third = words[2][here]
                groups = [slice(quarter * rows + g * eighth, quarter * rows + (g + 1) * eighth) for g in range(3)]
                tail = tail_lanes([words[2][group] for group in groups])
                for two in parts:
                    for g, group in enumerate(groups):
                        at_lane = 96 + 3 * two + g
                        tail = put(tail, at_lane, pltpu.roll(seconds[two][group], at_lane, 1))
                    tail = put(put(tail, 105 + 2 * two, tops[two]), 106 + 2 * two, highs[two])
                send_out[quad, pl.ds(pl.multiple_of(start, 8), rows)] = beside(words[0][here], third, 96)
                send_out[quad, pl.ds(pl.multiple_of(start + rows, 8), rows)] = beside(words[1][here], third, 64)
                send_out[quad, pl.ds(pl.multiple_of(start + 2 * rows, 8), eighth)] = tail
            for quarter in range(QUAD):
                start_one(quad, slot * QUAD + quarter, *outward)
            return carry

        lax.fori_loop(0, QUAD, one, 0)

    def outer(quad):
        wait_recv(quad, *outward)

        def across(first):
            return pl.ds(first, members, stride=block)

        tail = recv_out[quad, across(2 * rows)]
        scales = []
        for two in range(3):
            rest = size(tail[:, 105 + 2 * two : 106 + 2 * two].astype(jnp.float32)) * (1.0 / LEVELS)
            mean = size(tail[:, 106 + 2 * two : 107 + 2 * two].astype(jnp.float32)) * (1.0 / FINE)
            scales.append(jnp.where(lanes_of(tail) > 0, rest, mean))
        scale = jnp.concatenate(scales, axis=0)

        def some(step, carry):
            tails = [recv_out[quad, across(2 * rows + 2 * step + half)] for half in range(2)]
            values = []
            for g in range(3):
                both = []
                for half in range(2):
                    row = g * eighth + 2 * step + half
                    first, second = recv_out[quad, across(row)], recv_out[quad, across(rows + row)]
                    word = jnp.concatenate([first, second, third_of(first, second, tails[half], g)], axis=0)
                    apart = jnp.concatenate([pltpu.roll(tails[half], 32 - 3 * two - g, 1) for two in range(3)], axis=0)
                    both.append(jnp.concatenate(decode_apart(word, apart, scale), axis=0))
                values.append(jnp.concatenate(both, axis=1))
            mixed = [along_rows(value, row_ref[1]) for value in values]
            factors = [
                jnp.concatenate(
                    [kernel_ref[pl.ds(g * eighth + 2 * step + half, span, stride=rows)] for half in range(2)], axis=1
                )
                for g in range(3)
            ]
            restored = [along_rows(value * factor, row_ref[2]) for value, factor in zip(mixed, factors)]
            for half in range(2):
                side = slice(half * LANES, (half + 1) * LANES)
                words, tops = zip(*[encode(value[: span // 2, side], value[span // 2 :, side]) for value in restored])
                thirds = [word[2 * members :] for word in words]
                tail = tail_lanes(thirds)
                for g in range(3):
                    row = g * eighth + 2 * step + half
                    tail = put(tail, 96 + g, tops[g])
                    send_back[quad, across(row)] = beside(words[g][:members], thirds[g], 96)
                    send_back[quad, across(rows + row)] = beside(words[g][members : 2 * members], thirds[g], 64)
                send_back[quad, across(2 * rows + 2 * step + half)] = tail
            return carry

        lax.fori_loop(0, eighth // 2, some, 0)
        start_all(quad, *backward)

    def finish(quad):
        def one(step, carry):
            slot = lax.rem(my_slot + step, QUAD)
            source, wanted, often = task(quad, slot)
            weights = [jnp.where(wanted == side, often, 0.0) for side in range(2)]
            words, scales = [[], [], []], []
            for quarter in range(QUAD):
                wait_one(quad, slot * QUAD + quarter, *backward)
            for quarter in range(QUAD):
                start = (slot * QUAD + quarter) * block
                first, second = [
                    recv_back[quad, pl.ds(pl.multiple_of(start + two * rows, 8), rows)] for two in range(2)
                ]
                tail = recv_back[quad, pl.ds(pl.multiple_of(start + 2 * rows, 8), eighth)]
                words[0].append(first)
                words[1].append(second)
                for g in range(3):
                    group = slice(g * eighth, (g + 1) * eighth)
                    words[2].append(third_of(first[group], second[group], tail, g))
                    scales.append(tail[:, 96 + g : 97 + g])
            scale = size(jnp.concatenate(scales, axis=0).astype(jnp.float32)) * (1.0 / LEVELS) * undo_ref[...]
            parts = range(own_rows // 2)
            mixed = [jnp.concatenate(decode(jnp.concatenate(words[two], axis=0), scale), axis=1) for two in parts]
            mixed = [along_rows(value, row_ref[0]) for value in mixed]
            potentials = [
                along_lanes(jnp.concatenate([value[:, :LANES], value[:, LANES:]], axis=0), lane_ref[...]) for value in mixed
            ]
            for two in parts:
                part = pl.ds(2 * two * span, 2 * span)
                action = potentials[two] * unpack(window_part(source, two))
                for side in range(2):
                    total[side, part] += action * weights[side]
            return carry

        lax.fori_loop(0, QUAD, one, 0)

    total[...] = jnp.zeros_like(total)
    pl.semaphore_wait(barrier, members - 1)
    for quad in range(quads):
        inner(quad)
    kernel_copy.wait()
    for quad in range(quads):
        outer(quad)
    for quad in range(quads):
        finish(quad)

    swap = pltpu.make_async_remote_copy(
        src_ref=total.at[1 - core], dst_ref=partner_part, send_sem=part_sems.at[0], recv_sem=part_sems.at[1],
        device_id={"band": pair + 1 - core, "grid": lax.axis_index("grid")}, device_id_type=MESH,
    )
    swap.start()
    out_ref[core] = total[core]
    swap.wait_recv()
    out_ref[1 - core] = partner_part[...]
    swap.wait_send()
    for quad in range(quads):
        wait_send(quad, *outward)
        wait_send(quad, *backward)


def run_tasks(quads, span, members, *operands):
    own_rows = span // members
    whole = (quads, members * (span // QUAD) * 7 // 3, LANES)
    smem, vmem = pl.BlockSpec(memory_space=pltpu.SMEM), pl.BlockSpec(memory_space=pltpu.VMEM)
    sems = pltpu.SemaphoreType.DMA((quads, members))
    return pl.pallas_call(
        functools.partial(task_kernel, quads, span),
        out_shape=jax.ShapeDtypeStruct((2, own_rows * span, LANES), jnp.float32),
        in_specs=[smem] * 2 + [vmem] + [pl.BlockSpec(memory_space=pl.ANY)] + [vmem] * 3,
        out_specs=vmem,
        scratch_shapes=[pltpu.VMEM((span * span // QUAD, LANES), jnp.float32)]
        + [pltpu.VMEM(whole, jnp.int32)] * 4
        + [pltpu.VMEM((2, own_rows * span, LANES), jnp.float32), pltpu.VMEM((own_rows * span, LANES), jnp.float32)]
        + [sems] * 4
        + [pltpu.SemaphoreType.DMA((2,)), pltpu.SemaphoreType.DMA((1,))],
        compiler_params=pltpu.CompilerParams(
            collective_id=quads, has_side_effects=True, vmem_limit_bytes=56 * 1024 * 1024
        ),
        name="exchange_tasks",
    )(*operands)


def distinct_tasks(lists_ref, cap, chip):
    groups = lists_ref.shape[0]
    span = 2 * groups
    lane = lax.broadcasted_iota(jnp.int32, (groups, LANES), 1)
    live = lane < jnp.minimum(lists_ref[:, 2, :], cap)
    key = jnp.where(live, lists_ref[:, 1, :] * groups + lists_ref[:, 0, :], -1)
    per_row = LANES // span
    row_lane = lax.broadcasted_iota(jnp.int32, (1, LANES), 1)
    own = jnp.zeros((1, LANES), jnp.float32)
    most = jnp.zeros((1, 1), jnp.float32)
    for chunk in range(groups * groups // LANES):
        times = jnp.zeros((groups, LANES), jnp.float32)
        for slot in range(cap):
            times += jnp.where(key[:, slot : slot + 1] == lane + chunk * LANES, 1.0, 0.0)
        times = jnp.sum(times, axis=0, keepdims=True)
        for place in range(per_row):
            inside = (row_lane >= place * span) & (row_lane < (place + 1) * span)
            count = jnp.sum(jnp.where(inside & (times > 0.0), 1.0, 0.0), axis=1, keepdims=True)
            most = jnp.maximum(most, count)
            turned = pltpu.roll(times, (LANES - place * span) % LANES, 1) if place else times
            own += jnp.where((chip == chunk * per_row + place) & (row_lane < span), turned, 0.0)
    shape = (LANES, LANES)
    down, across = lax.broadcasted_iota(jnp.int32, shape, 0), lax.broadcasted_iota(jnp.int32, shape, 1)
    own_down = jnp.sum(jnp.where(down == across, own, 0.0), axis=1, keepdims=True)
    before = jnp.sum(jnp.where((across < down) & (own > 0.0), 1.0, 0.0), axis=1, keepdims=True)
    here = (before == across.astype(jnp.float32)) & (own_down > 0.0)
    entry = jnp.sum(jnp.where(here, down.astype(jnp.float32), 0.0), axis=0, keepdims=True)
    often = jnp.sum(jnp.where(here, own_down, 0.0), axis=0, keepdims=True)
    row = lax.broadcasted_iota(jnp.int32, (8, LANES), 0)
    return jnp.where(row == 0, entry, jnp.where(row == 1, often, most)).astype(jnp.int32)


def gather_kernel(
    rings, span, orbital_ref, slot_ref, pairs_ref, count_ref, window_ref, list_ref, lists_ref, give, own_list,
    swap_sems, list_send, list_recv, near_send, near_recv, far_send, far_recv,
):
    ring_x, ring_z = rings
    band = lax.axis_index("band")
    groups = lax.axis_size("band")
    core, chip = lax.rem(band, 2), band // 2
    at_x, at_z = chip // ring_z, lax.rem(chip, ring_z)
    packed = window_ref.shape[0] // groups

    barrier = pltpu.get_barrier_semaphore()

    def greet(step, carry):
        pl.semaphore_signal(barrier, inc=1, device_id={"band": lax.rem(band + step, groups)}, device_id_type=MESH)
        return carry

    lax.fori_loop(1, groups, greet, 0)

    part_rows = packed // 3
    quarter = part_rows // 3
    first = slot_ref[0] == 0
    for two in range(3):
        for side in range(2):
            rows = pl.ds(side * (orbital_ref.shape[1] // 2) + two * 4 * quarter, 4 * quarter)
            values = jnp.where(
                first, orbital_ref[0, rows].astype(jnp.float32), orbital_ref[1, rows].astype(jnp.float32)
            )
            last = values[3 * quarter :]
            for third in range(3):
                full = jnp.concatenate(
                    [values[third * quarter : (third + 1) * quarter], last[:, 32 * third : 32 * third + 32]], axis=1
                ).astype(jnp.bfloat16)
                row = two * part_rows + third * quarter

                @pl.when(core == side)
                def _():
                    window_ref[pl.ds(pl.multiple_of(band * packed + row, 16), quarter)] = full

                @pl.when(core != side)
                def _():
                    give[pl.ds(row, quarter)] = full

    own_list[...] = jnp.zeros_like(own_list)
    own_list[0:2, 0 : pairs_ref.shape[1]] = pairs_ref[...]
    own_list[2:3] = jnp.full((1, LANES), count_ref[0], jnp.int32)

    pl.semaphore_wait(barrier, groups - 1)

    def blocks(first_band, count):
        return window_ref.at[pl.ds(pl.multiple_of(first_band * packed, 16), count * packed)]

    def send(src, dst, send_sem, recv_sem, target):
        return pltpu.make_async_remote_copy(
            src_ref=src, dst_ref=dst, send_sem=send_sem, recv_sem=recv_sem,
            device_id={"band": target}, device_id_type=MESH,
        )

    def swap(owner):
        return send(give, blocks(owner, 1), swap_sems.at[0], swap_sems.at[1], band + 1 - 2 * core)

    swap(band).start()

    def send_list(step, owner):
        other = lax.rem(band + step, groups)
        return send(own_list, lists_ref.at[owner], list_send.at[step], list_recv.at[step], other)

    def start_list(step, carry):
        send_list(step, band).start()
        return carry

    def place(x, z):
        return lax.rem(x + ring_x, ring_x) * ring_z + lax.rem(z + ring_z, ring_z)

    level = (0, -1, 1, 2)
    later = packed // 9
    main, rest = (1, 0, 0, packed - later), (0, 1, packed - later, later)
    number = {main: 0, rest: 1}

    def along(plan, ring, step):
        move = [0, 0]
        if ring == 0:
            move[plan[0]] = step
        else:
            move[plan[1]], move[plan[0]] = step, level[ring - 1]
        return place(at_x + move[0], at_z + move[1])

    def neighbour(plan, ring, step):
        move = [0, 0]
        move[plan[min(ring, 1)]] = step
        return 2 * place(at_x + move[0], at_z + move[1]) + core

    def piece(plan, chip_at, half):
        return window_ref.at[pl.ds(pl.multiple_of((2 * chip_at + half) * packed + plan[2], 16), plan[3])]

    def near(plan, ring, way, half):
        block = piece(plan, along(plan, ring, 0), half)
        sems = [sem.at[number[plan], ring, way, half] for sem in (near_send, near_recv)]
        return send(block, block, *sems, neighbour(plan, ring, 1 - 2 * way))

    def far(plan, ring, way):
        block = piece(plan, along(plan, ring, -1 + 2 * way), way)
        sems = [sem.at[number[plan], ring, way] for sem in (far_send, far_recv)]
        return send(block, block, *sems, neighbour(plan, ring, 1 - 2 * way))

    def begin_half(plan, ring, half):
        for way in range(2):
            near(plan, ring, way, half).start()

    def begin(plan, ring):
        for turn in range(2):
            for way in range(2):
                near(plan, ring, way, way if turn == 0 else 1 - way).start()

    def onward(plan, ring, way):
        near(plan, ring, way, way).wait_recv()
        far(plan, ring, way).start()

    swap(band).wait_recv()
    begin(main, 0)
    begin(main, 1)
    begin(rest, 0)
    lax.fori_loop(1, groups, start_list, 0)
    for way in range(2):
        onward(main, 0, way)
        begin_half(main, 2 + way, way)
    for way in range(2):
        onward(rest, 0, way)
        onward(main, 1, way)
    for way in range(2):
        near(main, 0, way, 1 - way).wait_recv()
        begin_half(main, 2 + way, 1 - way)
    for way in range(2):
        far(main, 0, way).wait_recv()
        begin_half(main, 4, way)
    begin(rest, 1)
    for way in range(2):
        near(rest, 0, way, 1 - way).wait_recv()
        begin(rest, 2 + way)
    for turn in range(2):
        for way in range(2):
            onward(main, 2 + way, way if turn == 0 else 1 - way)
    for way in range(2):
        far(rest, 0, way).wait_recv()
    begin(rest, 4)
    for ring in range(1, 4):
        for way in range(2):
            onward(rest, ring, way)

    def end_list(step, carry):
        send_list(step, band).wait_recv()
        send_list(step, band).wait_send()
        return carry

    lax.fori_loop(1, groups, end_list, 0)
    lists_ref[band] = own_list[...]
    list_ref[...] = distinct_tasks(lists_ref, pairs_ref.shape[1], chip)

    for plan in (main, rest):
        for way in range(2):
            onward(plan, 4, way)
    for plan in (main, rest):
        for ring in range(1, 5):
            for way in range(2):
                near(plan, ring, way, 1 - way).wait_recv()
                far(plan, ring, way).wait_recv()
    swap(band).wait_send()
    for plan in (main, rest):
        for ring in range(5):
            for way in range(2):
                near(plan, ring, way, 0).wait_send()
                near(plan, ring, way, 1).wait_send()
                far(plan, ring, way).wait_send()


def gather_window(rings, span, orbitals, window_slot, task_pairs, task_count):
    groups = lax.axis_size("band")
    slab_rows = orbitals.shape[1]
    packed = slab_rows // 2 * span * span // LANES
    smem, vmem = pl.BlockSpec(memory_space=pltpu.SMEM), pl.BlockSpec(memory_space=pltpu.VMEM)
    dma = pltpu.SemaphoreType.DMA
    return pl.pallas_call(
        functools.partial(gather_kernel, rings, span),
        out_shape=(
            jax.ShapeDtypeStruct((groups * packed, LANES), jnp.bfloat16),
            jax.ShapeDtypeStruct((8, LANES), jnp.int32),
        ),
        in_specs=[vmem, smem, vmem, smem],
        out_specs=(vmem, vmem),
        scratch_shapes=[pltpu.VMEM((groups, 8, LANES), jnp.int32)]
        + [pltpu.VMEM((packed, LANES), jnp.bfloat16), pltpu.VMEM((8, LANES), jnp.int32)]
        + [dma((2,)), dma((groups,)), dma((groups,))]
        + [dma((2, 5, 2, 2))] * 2
        + [dma((2, 5, 2))] * 2,
        compiler_params=pltpu.CompilerParams(
            collective_id=9, has_side_effects=True, vmem_limit_bytes=56 * 1024 * 1024
        ),
        name="gather_window",
    )(orbitals.reshape(2, slab_rows * span, span), window_slot, task_pairs[0], task_count)


def on_device(orbitals, exchange_in, window_slot, task_pairs, task_count):
    band_dev, slab_rows, span, _ = orbitals.shape
    grid_parts = lax.axis_size("grid")
    groups = lax.axis_size("band")
    members = 2 * grid_parts
    own_rows = span // members
    window, lists = gather_window((4, 4), span, orbitals, window_slot, task_pairs, task_count)
    window = window.reshape(groups, -1, LANES)
    constants = [jnp.asarray(a) for a in (quarter_kernels(span), undo_emphasis(span), lane_table(span), row_tables(span))]
    most = lists[2, 0]

    def few():
        return run_tasks(3, span, members, jnp.zeros((1,), jnp.int32), lists, window, *constants)

    def many():
        def step(carry):
            start, total = carry
            return start + 16, total + run_tasks(4, span, members, start[None], lists, window, *constants)

        zero = jnp.zeros((2, own_rows * span, LANES), jnp.float32)
        return lax.while_loop(lambda carry: carry[0] < most, step, (jnp.int32(0), zero))[1]

    owned = lax.cond(most <= 12, few, many)
    owned = owned.reshape(slab_rows, span, LANES)[:, :, :span]
    slot_ids = jnp.arange(band_dev, dtype=jnp.int32)[:, None, None, None]
    return exchange_in + jnp.where(slot_ids == window_slot[0], owned, 0.0)


def solution(mesh):
    in_specs = (
        P("band", "grid", None, None),
        P("band", "grid", None, None),
        P("band"),
        P("band", None, None),
        P("band"),
    )
    out_specs = P("band", "grid", None, None)
    return jax.shard_map(
        on_device, mesh=mesh, in_specs=in_specs, out_specs=out_specs, check_vma=False
    )
```
